512 devices in a mesh: dp: 4 (over x), seq: 32 (over z_hi, y, core), tensor: 4 (over z_lo).
Axes of the slice: x: 4, y: 8, z: 8 (z_hi: 2, z_lo: 4; z = z_hi * 4 + z_lo), core: 2. Of those that a mesh axis runs over, the one named last changes fastest.
Arguments:
- query_rows: bfloat16 [16384, 3072], P(('dp', 'seq'), 'tensor'), parts along dimension 0, may hold values from -17 to 17
- key_rows: bfloat16 [16384, 3072], P(('dp', 'seq'), 'tensor'), parts along dimension 0, may hold values from -17 to 17
- value_rows: bfloat16 [16384, 3072], P(('dp', 'seq'), 'tensor'), parts along dimension 0, may hold values from -6 to 6
- deal_owner: int32 [16384], P(('dp', 'seq')), parts along dimension 0, may hold values from 0 to 31, as said below
- deal_slot: int32 [16384], P(('dp', 'seq')), parts along dimension 0, may hold values from 0 to 127
- clip_lengths: int32 [32], P('dp'), parts along dimension 0, may hold values from 1 to 1536, 4096 in all
- clip_steps: int32 [32], P('dp'), parts along dimension 0, may hold values from 0 to 999
- gate_table: bfloat16 [1000, 3072], P(None, 'tensor'), may hold values from -4 to 4
Outputs:
- attention_out: bfloat16 [16384, 3072], P(('dp', 'seq'), 'tensor'), parts along dimension 0
The draws below stay inside these ranges and needn't reach their ends.
There are 4 independent parts, one for each index of `dp`. The reference program is written for one: setup_inputs(seed, part) draws one part's arguments, and reference() takes and returns one part's arrays. A program takes and returns all parts, laid end to end along the dimension named above; an argument that names none is the same for every part. Nothing has to cross between parts.
Inputs may be any that keep to these rules, and one draw needn't show every extreme that they name: The pairs (deal_owner, deal_slot) are all distinct, so every owner receives exactly 128 rows; the rows of one device bound for one owner number at most 6, and that bound is reached in every draw.
All inputs are finite; a program needn't handle non-finite values.
Results may differ from the reference program's by a relative error of at most 0.0085.
Values may be sent and summed in bfloat16 or wider, within the bound.
No kernel may reach another device: no remote copies, remote signals or barrier semaphores. Data moves between devices by JAX's collectives and lax.ppermute only.
A program may use at most 64 MiB of HBM per device.

```python
import math
import jax
import jax.numpy as jnp
import numpy as np
from jax import lax

HEADS = 24
HEAD_DIM = 128
TOK_DEV = 128
CLIPS = 8
STEPS = 1000
TOKENS = 4096
MOST = 1536
N_SEQ = 32


def deal_tables(key):
    devices = N_SEQ
    per_device = TOK_DEV
    base_count = per_device // devices
    half_count = base_count // 2
    subkeys = jax.random.split(key, 4)
    first_pick = jax.random.permutation(subkeys[0], devices).astype(jnp.int32)
    offset = jax.random.randint(subkeys[1], (), 1, devices, dtype=jnp.int32)
    second_pick = (first_pick + offset) % devices
    owner_ids = jnp.arange(devices, dtype=jnp.int32)
    raised = (owner_ids[None, :] == first_pick[:, None]).astype(jnp.int32)
    lowered = (owner_ids[None, :] == second_pick[:, None]).astype(jnp.int32)
    counts = base_count + half_count * raised - half_count * lowered
    send_ends = jnp.cumsum(counts, axis=1).astype(jnp.int32)
    send_starts = send_ends - counts
    positions = jnp.arange(per_device, dtype=jnp.int32)
    sorted_owner = jnp.sum((send_ends[:, None, :] <= positions[None, :, None]).astype(jnp.int32), axis=2).astype(jnp.int32)
    within = positions[None, :] - jnp.take_along_axis(send_starts, sorted_owner, axis=1)
    receive_ends = jnp.cumsum(counts.T, axis=1).astype(jnp.int32)
    receive_starts = receive_ends - counts.T
    sources = jnp.broadcast_to(owner_ids[:, None], (devices, per_device))
    arrival_place = receive_starts[sorted_owner, sources] + within
    slot_order = jax.vmap(lambda subkey: jax.random.permutation(subkey, per_device))(jax.random.split(subkeys[2], devices)).astype(jnp.int32)
    sorted_slot = slot_order[sorted_owner, arrival_place]
    row_order = jax.vmap(lambda subkey: jax.random.permutation(subkey, per_device))(jax.random.split(subkeys[3], devices)).astype(jnp.int32)
    owner_table = jnp.take_along_axis(sorted_owner, row_order, axis=1)
    slot_table = jnp.take_along_axis(sorted_slot, row_order, axis=1)
    return (owner_table.reshape(-1).astype(jnp.int32), slot_table.reshape(-1).astype(jnp.int32))


def draw_deal_owner(key, part):
    owner_table, slot_table = deal_tables(key)
    return owner_table


def draw_deal_slot(key, part):
    owner_table, slot_table = deal_tables(key)
    return slot_table


def draw_query_rows(key, part):
    key = jax.random.fold_in(key, 11)
    first_key = jax.random.fold_in(key, 0)
    row_width = HEADS * HEAD_DIM
    values = jnp.clip(jax.random.normal(first_key, (TOKENS, row_width), jnp.float32), -6.0, 6.0)
    return values.astype(jnp.bfloat16)


def draw_key_rows(key, part):
    key = jax.random.fold_in(key, 12)
    first_key = jax.random.fold_in(key, 0)
    row_width = HEADS * HEAD_DIM
    values = jnp.clip(jax.random.normal(first_key, (TOKENS, row_width), jnp.float32), -6.0, 6.0)
    return values.astype(jnp.bfloat16)


def touch_ends(drawn, rng, low, top_value):
    longest = drawn.shape.index(max(drawn.shape))
    spots = []
    for shift in (0, 1):
        where = [jax.random.randint(jax.random.fold_in(rng, axis), (), 0, length) for axis, length in enumerate(drawn.shape)]
        where[longest] = (where[longest] + shift) % drawn.shape[longest]
        spots.append(tuple(where))
    return drawn.at[spots[0]].set(low).at[spots[1]].set(top_value)


def levels(rng, dims, pieces, smallest, high):
    def one(axis_at, blocks):
        draws = jax.random.uniform(jax.random.fold_in(jax.random.fold_in(rng, 6), axis_at), (blocks,), jnp.float32, smallest / len(pieces), high / len(pieces))
        return jnp.repeat(jnp.exp(draws), dims[axis_at] // blocks).reshape((-1,) + (1,) * (len(dims) - axis_at - 1))

    loudness = one(*pieces[0])
    for cut in pieces[1:]:
        loudness = loudness * one(*cut)
    return loudness


def length_profile(count, total, limit, slope):
    loads = [(1 << 20) // math.isqrt(grade ** slope) + 1 for grade in range(2, count + 1)]
    surplus, holding = total - limit - (count - 1), [1] * (count - 1)
    while surplus > 0:
        movable = [i for i in range(count - 1) if holding[i] < limit]
        pool, budget = sum([loads[i] for i in movable]), surplus
        for i in movable:
            extra = min(limit - holding[i], max(1, budget * loads[i] // pool), surplus)
            holding[i] = holding[i] + extra
            surplus = surplus - extra
    return np.array([limit] + holding)


def ragged(rng, number_of, total, reach, slope):
    if number_of == 2:
        one = jax.random.randint(rng, (), max(1, total - reach), min(reach, total - 1) + 1)
        return jnp.stack([one, total - one])
    lengths = jnp.asarray(length_profile(number_of, total, reach, slope), jnp.int32)
    pairs = (number_of - 1) // 2
    donor, taker = lengths[1:1 + 2 * pairs:2], lengths[2:2 + 2 * pairs:2]
    margin = jnp.minimum(donor - 1, reach - taker)
    shifted = jax.random.randint(jax.random.fold_in(rng, 1), (pairs,), 0, 1 << 20) % (margin + 1)
    lengths = lengths.at[1:1 + 2 * pairs:2].set(donor - shifted).at[2:2 + 2 * pairs:2].set(taker + shifted)
    return lengths[jax.random.permutation(jax.random.fold_in(rng, 2), number_of)]


def scatter_about(own_key, dims, scale, reach, cuts=(), held_as=jnp.bfloat16):
    drawn = jax.random.normal(own_key, dims, jnp.float32) * scale
    if len(cuts) > 0:
        drawn = levels(own_key, dims, cuts, -0.22, 0.18) * drawn
    return jnp.clip(drawn, min=-reach, max=reach).astype(held_as)


def setup_inputs(seed: int = 0, part: int = 0) -> dict:
    key_of = jax.random.split(jax.random.key(seed), 9)
    part_splits = jax.random.split(jax.random.fold_in(key_of[8], part), 9)
    return {
        "query_rows": draw_query_rows(jax.random.fold_in(jax.random.fold_in(key_of[8], part), 71), part),
        "key_rows": draw_key_rows(jax.random.fold_in(jax.random.fold_in(key_of[8], part), 71), part),
        "value_rows": scatter_about(part_splits[2], (TOKENS, HEADS * HEAD_DIM), 1.0, 6.0, ((0, 32), (1, 4))),
        "deal_owner": draw_deal_owner(jax.random.fold_in(jax.random.fold_in(key_of[8], part), 71), part),
        "deal_slot": draw_deal_slot(jax.random.fold_in(jax.random.fold_in(key_of[8], part), 71), part),
        "clip_lengths": ragged(part_splits[5], CLIPS, TOKENS, MOST, 2).astype(jnp.int32),
        "clip_steps": touch_ends(jax.random.randint(part_splits[6], (CLIPS,), 0, STEPS), jax.random.fold_in(part_splits[6], 1), 0, STEPS - 1).astype(jnp.int32),
        "gate_table": scatter_about(key_of[7], (STEPS, HEADS * HEAD_DIM), 1.0, 4.0, ((1, 4),)),
    }


masked_score = -1e+30

def clip_index(positions, clip_lengths):
    clip_ends = jnp.cumsum(clip_lengths).astype(jnp.int32)
    return lax.optimization_barrier(jnp.sum((clip_ends[None, :] <= positions[:, None]).astype(jnp.int32), axis=1)).astype(jnp.int32)

def reference(query_rows, key_rows, value_rows, deal_owner, deal_slot, clip_lengths, clip_steps, gate_table):
    total_rows = query_rows.shape[0]
    row_width = query_rows.shape[1]
    head_count = row_width // HEAD_DIM
    per_device = total_rows // N_SEQ
    placed = (deal_owner * per_device + deal_slot).astype(jnp.int32)

    def arrange(source):
        packed = jnp.zeros_like(source).at[placed].set(source)
        return packed.reshape(total_rows, head_count, HEAD_DIM).transpose(1, 0, 2)
    packed_query = arrange(query_rows)
    packed_key = arrange(key_rows)
    packed_value = arrange(value_rows)
    positions = jnp.arange(total_rows, dtype=jnp.int32)
    clip_ids = clip_index(positions, clip_lengths)
    same_clip = clip_ids[:, None] == clip_ids[None, :]
    score_scale = 1.0 / math.sqrt(HEAD_DIM)

    def one_head(operands):
        head_query, head_key, head_value = operands
        scores = jnp.dot(head_query, head_key.T, preferred_element_type=jnp.float32) * score_scale
        row_top = lax.optimization_barrier(jnp.max(jnp.where(same_clip, scores, masked_score), axis=1, keepdims=True))
        raw_weights = jnp.where(same_clip, jnp.exp(scores - row_top), 0.0)
        row_total = lax.optimization_barrier(jnp.sum(raw_weights, axis=1, keepdims=True))
        numerator = jnp.dot(raw_weights.astype(jnp.bfloat16), head_value, preferred_element_type=jnp.float32)
        return numerator / row_total
    attended = lax.map(one_head, (packed_query, packed_key, packed_value))
    attended = attended.transpose(1, 0, 2).reshape(total_rows, row_width)
    gate_rows = gate_table[clip_steps[clip_ids]].astype(jnp.float32)
    return (attended * gate_rows).astype(jnp.bfloat16)
```

```python
import functools
import math

import jax
import jax.numpy as jnp
from jax import lax
from jax.experimental import pallas as pl
from jax.experimental.pallas import tpu as pltpu
from jax.sharding import PartitionSpec as P

HEAD_DIM = 128
MASKED = -1e30
SCALE = 1.0 / math.sqrt(HEAD_DIM)
LOG2E = math.log2(math.e)
ROWS_BOUND = 6
MSG = 8
CHUNK = 256

NT = (((1,), (1,)), ((), ()))
TN = (((0,), (0,)), ((), ()))


def iota(shape, axis):
    return lax.broadcasted_iota(jnp.int32, shape, axis)


def dot(a, b, dims=(((1,), (0,)), ((), ()))):
    return lax.dot_general(a, b, dims, preferred_element_type=jnp.float32)


def clip_bounds(lengths_ref):
    bounds = []
    end = jnp.int32(0)
    for c in range(lengths_ref.shape[0]):
        start = end
        end = end + lengths_ref[c]
        bounds.append((start, end))
    return bounds


def pack_kernel(owners, lengths_ref, owner_ref, slot_ref, query_ref, out_ref):
    rows = query_ref.shape[0]
    owner = owner_ref[...]
    slot = slot_ref[...]
    place = owner * rows + slot
    clip = jnp.zeros_like(place)
    for _, end in clip_bounds(lengths_ref):
        clip = clip + (place >= end).astype(jnp.int32)
    along = jnp.broadcast_to(owner.astype(jnp.float32), (rows, rows))
    down = along.T
    earlier = (along == down) & (iota((rows, rows), 0) < iota((rows, rows), 1))
    rank = jnp.sum(earlier.astype(jnp.float32), axis=0, keepdims=True)
    rank_down = jnp.broadcast_to(rank, (rows, rows)).T
    target = owner * MSG + rank.astype(jnp.int32)
    spread = (owners * MSG, rows)
    line = iota(spread, 0)
    kind = lax.rem(line, MSG)
    pick = (line == target).astype(jnp.bfloat16)
    main = dot(pick, query_ref[...])
    slot_part = jnp.where(
        (kind == ROWS_BOUND) & (lax.div(line, MSG) == owner), (slot + 1).astype(jnp.float32), 0.0
    ).astype(jnp.bfloat16)
    rank_at = (rank_down == iota((rows, rows), 1).astype(jnp.float32)).astype(jnp.bfloat16)
    clip_part = jnp.where(kind == ROWS_BOUND + 1, clip.astype(jnp.float32), 0.0).astype(jnp.bfloat16)
    unit = (iota((rows, rows), 0) == iota((rows, rows), 1)).astype(jnp.bfloat16)
    extra = dot(slot_part, rank_at) + dot(clip_part, unit)
    out_ref[...] = main.astype(jnp.bfloat16)
    out_ref[:, :rows] = (main[:, :rows] + extra).astype(jnp.bfloat16)


def unpack_kernel(owners, plane, plane_ref, got_ref, query_ref, key_clip_ref):
    lines = owners * MSG
    rows = query_ref.shape[0]
    got = got_ref[...]
    head = got[:, :rows]
    square = (lines, lines)
    to_slot = (lax.div(iota(square, 0), MSG) * MSG + ROWS_BOUND == iota(square, 1)).astype(
        jnp.bfloat16
    )
    spread = dot(to_slot, head)
    kind = lax.rem(iota((lines, rows), 0), MSG)
    lane = iota((lines, rows), 1)
    place = jnp.sum(
        jnp.where((lane == kind) & (kind < ROWS_BOUND), spread, 0.0), axis=1, keepdims=True
    )
    put = (place == (lane + 1).astype(jnp.float32)).astype(jnp.bfloat16)
    query_ref[...] = dot(put, got, TN).astype(jnp.bfloat16)
    first = plane_ref[0] * plane
    block = (plane, lines)
    to_clip = (
        (iota(block, 0) + first) * MSG + ROWS_BOUND + 1 == iota(block, 1)
    ).astype(jnp.bfloat16)
    clips = dot(to_clip, head)
    unit = (iota((rows, rows), 0) == iota((rows, rows), 1)).astype(jnp.bfloat16)
    down = iota((rows, rows), 0).astype(jnp.float32)
    for j in range(plane):
        member = (clips[j : j + 1, :] == down).astype(jnp.bfloat16)
        key_clip_ref[j * rows : (j + 1) * rows, :] = dot(unit, member, NT).astype(jnp.bfloat16)


def attend_kernel(
    base_ref, lengths_ref, query_ref, key_ref, value_ref, key_clip_ref, out_ref, stat_ref, scores
):
    h = pl.program_id(0)
    rows = query_ref.shape[0]
    keys = key_ref.shape[0]
    position = iota((rows, HEAD_DIM), 0) + base_ref[0]
    lane = iota((rows, HEAD_DIM), 1)
    dead = jnp.zeros((rows, HEAD_DIM), jnp.float32)
    for c, (start, end) in enumerate(clip_bounds(lengths_ref)):
        outside = (position < start) | (position >= end)
        dead = jnp.where((lane == c) & outside, MASKED, dead)
    query = jnp.concatenate([query_ref[...], dead.astype(jnp.bfloat16)], axis=1)
    top = jnp.full((rows, HEAD_DIM), -3e38, jnp.float32)
    for k in range(0, keys, CHUNK):
        key = jnp.concatenate(
            [key_ref[k : k + CHUNK, :], key_clip_ref[k : k + CHUNK, :]], axis=1
        )
        s = dot(query, key, NT)
        scores[:, k : k + CHUNK] = s
        for j in range(0, CHUNK, HEAD_DIM):
            top = jnp.maximum(top, s[:, j : j + HEAD_DIM])
    top = jnp.max(top, axis=1, keepdims=True)
    shift = top * (SCALE * LOG2E)
    ones = jnp.ones((CHUNK, HEAD_DIM), jnp.bfloat16)
    total = jnp.zeros((rows, 2 * HEAD_DIM), jnp.float32)
    for k in range(0, keys, CHUNK):
        w = jnp.exp2(scores[:, k : k + CHUNK] * (SCALE * LOG2E) - shift).astype(jnp.bfloat16)
        value = jnp.concatenate([value_ref[k : k + CHUNK, :], ones], axis=1)
        total = total + dot(w, value)
    weight = total[:, HEAD_DIM:]
    out_ref[...] = (total[:, :HEAD_DIM] / weight).astype(out_ref.dtype)
    level = shift + jnp.log2(weight)

    high = level.astype(jnp.bfloat16)
    rest = level - high.astype(jnp.float32)
    mid = rest.astype(jnp.bfloat16)
    low = (rest - mid.astype(jnp.float32)).astype(jnp.bfloat16)
    held = jnp.where(h == 0, jnp.zeros((rows, HEAD_DIM), jnp.bfloat16), stat_ref[...])
    held = jnp.where(lane == h, high, held)
    held = jnp.where(lane == h + 8, mid, held)
    stat_ref[...] = jnp.where(lane == h + 16, low, held)


def combine_kernel(
    base_ref, lengths_ref, own_ref, own_stat_ref, far_ref, gates_ref, out_ref
):
    rows, width = own_ref.shape
    position = iota((rows, HEAD_DIM), 0) + base_ref[0]
    lane = iota((rows, HEAD_DIM), 1)
    member = jnp.zeros((rows, HEAD_DIM), jnp.float32)
    for c, (start, end) in enumerate(clip_bounds(lengths_ref)):
        inside = (position >= start) & (position < end)
        member = jnp.where((lane == c) & inside, 1.0, member)
    gate = dot(member[:, : gates_ref.shape[0]].astype(jnp.bfloat16), gates_ref[...])

    own_stat = own_stat_ref[...].astype(jnp.float32)
    far_stat = far_ref[:, width:].astype(jnp.float32)
    for h in range(width // HEAD_DIM):

        def level(stat):
            return (stat[:, h : h + 1] + stat[:, h + 8 : h + 9]) + stat[:, h + 16 : h + 17]

        gap = level(own_stat) - level(far_stat)
        own_share = 1.0 / (1.0 + jnp.exp2(-gap))
        far_share = 1.0 / (1.0 + jnp.exp2(gap))
        at = slice(h * HEAD_DIM, (h + 1) * HEAD_DIM)
        mixed = own_ref[:, at] * own_share + far_ref[:, at].astype(jnp.float32) * far_share
        out_ref[:, at] = (mixed * gate[:, at]).astype(jnp.bfloat16)


SMEM = pl.BlockSpec(memory_space=pltpu.SMEM)
VMEM = pl.BlockSpec(memory_space=pltpu.VMEM)


def attend(base, lengths, query, key_value, key_clip, out_type):
    rows, width = query.shape
    heads = width // HEAD_DIM
    keys = key_value.shape[0]
    return pl.pallas_call(
        attend_kernel,
        grid=(heads,),
        in_specs=[
            SMEM,
            SMEM,
            pl.BlockSpec((rows, HEAD_DIM), lambda h: (0, h)),
            pl.BlockSpec((keys, HEAD_DIM), lambda h: (0, h)),
            pl.BlockSpec((keys, HEAD_DIM), lambda h: (0, heads + h)),
            pl.BlockSpec((keys, HEAD_DIM), lambda h: (0, 0)),
        ],
        out_specs=[
            pl.BlockSpec((rows, HEAD_DIM), lambda h: (0, h)),
            pl.BlockSpec((rows, HEAD_DIM), lambda h: (0, 0)),
        ],
        out_shape=[
            jax.ShapeDtypeStruct((rows, width), out_type),
            jax.ShapeDtypeStruct((rows, HEAD_DIM), jnp.bfloat16),
        ],
        scratch_shapes=[pltpu.VMEM((rows, keys), jnp.float32)],
        compiler_params=pltpu.CompilerParams(vmem_limit_bytes=32 * 1024 * 1024),
        cost_estimate=pl.CostEstimate(
            flops=4 * rows * keys * width,
            bytes_accessed=4 * keys * width,
            transcendentals=rows * keys * heads,
        ),
    )(base, lengths, query, key_value, key_value, key_clip)


def shards(
    query_rows, key_rows, value_rows, deal_owner, deal_slot, clip_lengths, clip_steps, gate_table
):
    devices = lax.axis_size("seq")
    plane = devices // 2
    rows, width = query_rows.shape
    me = lax.axis_index("seq")
    far = (me + plane) % devices
    across = [(i, (i + plane) % devices) for i in range(devices)]
    planes = [list(range(plane)), list(range(plane, devices))]

    key_value = lax.all_gather(
        jnp.concatenate([key_rows, value_rows], axis=1),
        "seq",
        axis_index_groups=planes,
        tiled=True,
    )

    message = pl.pallas_call(
        functools.partial(pack_kernel, devices),
        in_specs=[SMEM, VMEM, VMEM, VMEM],
        out_specs=VMEM,
        out_shape=jax.ShapeDtypeStruct((devices * MSG, width), jnp.bfloat16),
    )(clip_lengths, deal_owner[None, :], deal_slot[None, :], query_rows)
    got = lax.all_to_all(
        message.reshape(devices, MSG, width), "seq", split_axis=0, concat_axis=0, tiled=True
    ).reshape(devices * MSG, width)
    query, key_clip = pl.pallas_call(
        functools.partial(unpack_kernel, devices, plane),
        in_specs=[SMEM, VMEM],
        out_specs=[VMEM, VMEM],
        out_shape=[
            jax.ShapeDtypeStruct((rows, width), jnp.bfloat16),
            jax.ShapeDtypeStruct((plane * rows, HEAD_DIM), jnp.bfloat16),
        ],
    )((me // plane)[None], got)
    far_query = lax.ppermute(query, "seq", across)
    gates = jnp.take(gate_table, clip_steps, axis=0)

    base = (me * rows)[None]
    far_base = (far * rows)[None]
    far_out, far_stat = attend(
        far_base, clip_lengths, far_query, key_value, key_clip, jnp.bfloat16
    )
    sent = lax.ppermute(jnp.concatenate([far_out, far_stat], axis=1), "seq", across)
    own_out, own_stat = attend(base, clip_lengths, query, key_value, key_clip, jnp.float32)
    return pl.pallas_call(
        combine_kernel,
        in_specs=[SMEM, SMEM, VMEM, VMEM, VMEM, VMEM],
        out_specs=VMEM,
        out_shape=jax.ShapeDtypeStruct((rows, width), jnp.bfloat16),
    )(base, clip_lengths, own_out, own_stat, sent, gates)


def solution(mesh):
    placed = (
        P(("dp", "seq"), "tensor"),
        P(("dp", "seq"), "tensor"),
        P(("dp", "seq"), "tensor"),
        P(("dp", "seq")),
        P(("dp", "seq")),
        P("dp"),
        P("dp"),
        P(None, "tensor"),
    )
    return jax.shard_map(
        shards, mesh=mesh, in_specs=placed, out_specs=P(("dp", "seq"), "tensor"), check_vma=False
    )
```

```python
import functools
import math

import jax
import jax.numpy as jnp
from jax import lax
from jax.experimental import pallas as pl
from jax.experimental.pallas import tpu as pltpu
from jax.sharding import PartitionSpec as P

HEAD_DIM = 128
MASKED = -1e30
SCALE2 = math.log2(math.e) / math.sqrt(HEAD_DIM)
BOUND = 6
MSG = 24
CHUNK = 256
ATTEND_VMEM = 24 * 1024 * 1024
SMALL_VMEM = 10 * 1024 * 1024

NN = (((1,), (0,)), ((), ()))
NT = (((1,), (1,)), ((), ()))
TN = (((0,), (0,)), ((), ()))


def iota(shape, axis):
    return lax.broadcasted_iota(jnp.int32, shape, axis)


def dot(a, b, dims=NN):
    return lax.dot_general(a, b, dims, preferred_element_type=jnp.float32)


def unit(size):
    return (iota((size, size), 0) == iota((size, size), 1)).astype(jnp.bfloat16)


def clip_bounds(lengths_ref):
    bounds = []
    end = jnp.int32(0)
    for c in range(lengths_ref.shape[0]):
        start = end
        end = end + lengths_ref[c]
        bounds.append((start, end))
    return bounds


def split_kernel(devices, me_ref, key_ref, value_ref, kept_ref, given_ref):
    half = key_ref.shape[1] // 2
    low, high = slice(0, half), slice(half, 2 * half)
    side = place_of(me_ref[0], devices)[0]

    @pl.when(side == 0)
    def _():
        kept_ref[:, low] = key_ref[:, low]
        kept_ref[:, high] = value_ref[:, low]
        given_ref[:, low] = key_ref[:, high]
        given_ref[:, high] = value_ref[:, high]

    @pl.when(side != 0)
    def _():
        kept_ref[:, low] = key_ref[:, high]
        kept_ref[:, high] = value_ref[:, high]
        given_ref[:, low] = key_ref[:, low]
        given_ref[:, high] = value_ref[:, low]


def pack_kernel(plane, lengths_ref, owner_ref, slot_ref, query_ref, out_ref):
    rows, width = query_ref.shape
    half = width // 2
    ring = plane // 2
    owner = owner_ref[...]
    slot = slot_ref[...]
    place = owner * rows + slot
    clip = jnp.zeros_like(place)
    for _, end in clip_bounds(lengths_ref):
        clip = clip + (place >= end).astype(jnp.int32)
    clip = jnp.broadcast_to(clip.astype(jnp.float32), (8, rows))
    square = (rows, rows)
    along = jnp.broadcast_to(owner.astype(jnp.float32), square)
    earlier = (along == along.T) & (iota(square, 0) < iota(square, 1))
    rank = jnp.sum(earlier.astype(jnp.float32), axis=0, keepdims=True).astype(jnp.int32)
    there = lax.div(lax.rem(owner, plane), 2)
    which = lax.div(owner, plane) * 2 + lax.rem(owner, 2)
    target = there * MSG + which * BOUND + rank
    spread = (ring * MSG, rows)
    line = iota(spread, 0)
    lane = iota(spread, 1)
    kind = lax.rem(line, MSG)
    pick = (line == target).astype(jnp.bfloat16)
    main = dot(pick, query_ref[...])
    slot_down = jnp.broadcast_to((slot + 1).astype(jnp.float32), square).T
    slots = jnp.where(iota(square, 1) == rows - 1, slot_down, 0.0).astype(jnp.bfloat16)
    meta = dot(pick, slots)
    meta = jnp.where((kind == 0) & (lane < rows // 2), clip[:1], meta)
    turned = pltpu.roll(clip, rows // 2, 1)[:1]
    meta = jnp.where((kind == 1) & (lane < rows // 2), turned, meta).astype(jnp.bfloat16)
    for s in range(2):
        at = slice(s * ring * MSG, (s + 1) * ring * MSG)
        out_ref[at, :half] = main[:, s * half : (s + 1) * half].astype(jnp.bfloat16)
        out_ref[at, half:] = meta


def place_of(me, devices):
    plane = devices // 2
    half = lax.div(me, plane)
    return half, lax.div(lax.rem(me, plane), 2), lax.rem(me, 2)


def key_sources(me, devices):
    plane = devices // 2
    ring = plane // 2
    half, y, core = place_of(me, devices)

    def pair(h, distance):
        there = lax.rem(y + (2 * core - 1) * distance + ring, ring)
        at = h * plane + there * 2
        return [at, at + 1]

    near, far = half, 1 - half
    order = [me, lax.rem(me + plane, devices)]
    for h, distance in ((near, 1), (near, 2), (far, 1), (near, 3), (far, 2), (far, 3)):
        order += pair(h, distance)
    return order + [pair(near, 4)[0] + core, pair(far, 4)[0] + core]


def unpack_kernel(
    devices,
    early,
    me_ref,
    lengths_ref,
    got_ref,
    other_ref,
    query_ref,
    other_query_ref,
    clips0_ref,
    clips1_ref,
    dead_ref,
):
    each = got_ref.shape[0]
    lines = 2 * each
    rows = HEAD_DIM
    plane = devices // 2
    me = me_ref[0]
    half, _, core = place_of(me, devices)
    got = jnp.concatenate([got_ref[...], other_ref[...]], axis=0)
    data, meta = got[:, :-rows], got[:, -rows:]
    kind = lax.rem(iota((lines, 1), 0), MSG)
    from_half = lax.div(kind, 2 * BOUND)
    from_core = lax.rem(lax.div(kind, BOUND), 2)
    quarter = (from_core != core).astype(jnp.int32) * 2 + (from_half != half).astype(jnp.int32)
    slot = meta[:, rows - 1 :].astype(jnp.float32)
    target = jnp.where(slot > 0, slot - 1.0 + (quarter * rows).astype(jnp.float32), -1.0)
    target = jnp.broadcast_to(target, (lines, rows))
    target = jnp.concatenate(
        [target[i : i + rows, :].T[:1, :] for i in range(0, lines, rows)], axis=1
    )
    put = (iota((4 * rows, lines), 0).astype(jnp.float32) == target).astype(jnp.bfloat16)
    queries = dot(put, data).astype(jnp.bfloat16)
    query_ref[...] = queries[: 2 * rows]
    other_query_ref[...] = queries[2 * rows :]

    order = key_sources(me, devices)
    slots = len(order)
    block = (slots, lines)
    line = iota(block, 0)
    source = jnp.zeros(block, jnp.int32)
    for j, at in enumerate(order):
        at = lax.div(at, 2) * MSG + (lax.rem(at, 2) != core).astype(jnp.int32) * each
        source = jnp.where(line == j, at, source)
    first = dot((source == iota(block, 1)).astype(jnp.bfloat16), meta)
    second = dot((source + 1 == iota(block, 1)).astype(jnp.bfloat16), meta)
    ids = jnp.where(iota((slots, rows), 1) < rows // 2, first, pltpu.roll(second, rows // 2, 1))
    down = iota((rows, rows), 0).astype(jnp.float32)
    for j in range(slots):
        member = (ids[j : j + 1, :] == down).astype(jnp.bfloat16)
        clips = dot(unit(rows), member, NT).astype(jnp.bfloat16)
        if j < early:
            clips0_ref[j * rows : (j + 1) * rows, :] = clips
        else:
            clips1_ref[(j - early) * rows : (j + 1 - early) * rows, :] = clips

    bounds = clip_bounds(lengths_ref)
    other = lax.rem(me + plane, devices)
    away = 1 - 2 * core
    lane = iota((rows, HEAD_DIM), 1)
    for q, owner in enumerate((me, other, me + away, other + away)):
        position = iota((rows, HEAD_DIM), 0) + owner * rows
        dead = jnp.zeros((rows, HEAD_DIM), jnp.float32)
        for c, (start, end) in enumerate(bounds):
            outside = (position < start) | (position >= end)
            dead = jnp.where((lane == c) & outside, MASKED, dead)
        dead_ref[q * rows : (q + 1) * rows, :] = dead.astype(jnp.bfloat16)


def split3(value):
    high = value.astype(jnp.bfloat16)
    rest = value - high.astype(jnp.float32)
    mid = rest.astype(jnp.bfloat16)
    low = (rest - mid.astype(jnp.float32)).astype(jnp.bfloat16)
    return high, mid, low


def pair_up(sizes):
    chunks = []
    at = 0
    parts = []
    for i, size in enumerate(sizes):
        if size >= CHUNK:
            for start in range(0, size, CHUNK):
                chunks.append((at, [(i, start, CHUNK)]))
                at += CHUNK
            continue
        parts.append((i, 0, size))
        if sum(p[2] for p in parts) == CHUNK:
            chunks.append((at, parts))
            at += CHUNK
            parts = []
    assert not parts
    return chunks


def attend_kernel(sizes, first, last, *refs):
    refs = list(refs)
    dead_ref = refs.pop(0)
    query_refs = [refs.pop(0), refs.pop(0)]
    block_refs = [refs.pop(0) for _ in sizes]
    clip_ref = refs.pop(0)
    if not first:
        sum_ref, stat_ref = refs.pop(0), refs.pop(0)
    if last:
        out_ref, level_ref, sent_ref = refs.pop(0), refs.pop(0), refs.pop(0)
    else:
        new_sum_ref, new_stat_ref = refs.pop(0), refs.pop(0)
    scores = refs.pop(0)
    tile, width = query_refs[0].shape
    heads = width // HEAD_DIM
    lane = iota((tile, HEAD_DIM), 1)
    chunks = pair_up(sizes)
    ones = jnp.ones((CHUNK, HEAD_DIM), jnp.bfloat16)
    for t in range(2):
        rows = slice(t * tile, (t + 1) * tile)
        stat = jnp.zeros((tile, HEAD_DIM), jnp.float32)
        for h in range(heads):
            key_at = slice(h * HEAD_DIM, (h + 1) * HEAD_DIM)
            value_at = slice(width + h * HEAD_DIM, width + (h + 1) * HEAD_DIM)
            query = jnp.concatenate([query_refs[t][:, key_at], dead_ref[rows, :]], axis=1)
            top = jnp.full((tile, HEAD_DIM), -3e38, jnp.float32)
            for at, members in chunks:
                key = jnp.concatenate([block_refs[i][o : o + n, key_at] for i, o, n in members])
                key = jnp.concatenate([key, clip_ref[at : at + CHUNK, :]], axis=1)
                s = dot(query, key, NT)
                scores[t * heads + h, :, at : at + CHUNK] = s
                for j in range(0, CHUNK, HEAD_DIM):
                    top = jnp.maximum(top, s[:, j : j + HEAD_DIM])
            top = jnp.max(top, axis=1, keepdims=True) * SCALE2
            if first:
                total = jnp.zeros((tile, 2 * HEAD_DIM), jnp.float32)
            else:
                old_top = stat_ref[rows, h : h + 1]
                top = jnp.maximum(top, old_top)
                fade = jnp.exp2(old_top - top)
                weight = stat_ref[rows, h + 8 : h + 9] * fade
                weight = jnp.broadcast_to(weight, (tile, HEAD_DIM))
                total = jnp.concatenate([sum_ref[rows, key_at] * fade, weight], axis=1)
            for at, members in chunks:
                w = scores[t * heads + h, :, at : at + CHUNK] * SCALE2 - top
                w = jnp.exp2(w).astype(jnp.bfloat16)
                value = jnp.concatenate([block_refs[i][o : o + n, value_at] for i, o, n in members])
                total = total + dot(w, jnp.concatenate([value, ones], axis=1))
            weight = total[:, HEAD_DIM:]
            if not last:
                new_sum_ref[rows, key_at] = total[:, :HEAD_DIM]
                stat = jnp.where(lane == h, top, stat)
                stat = jnp.where(lane == h + 8, weight, stat)
                continue
            out = total[:, :HEAD_DIM] / weight
            stat = jnp.where(lane == h, top + jnp.log2(weight), stat)
            if t == 0:
                out_ref[:, key_at] = out
            else:
                sent_ref[:, key_at] = out.astype(jnp.bfloat16)
        if not last:
            new_stat_ref[rows, :] = stat
        elif t == 0:
            level_ref[...] = stat
        else:
            high, mid, low = split3(stat)
            mid = pltpu.roll(mid.astype(jnp.float32), 8, 1)
            low = pltpu.roll(low.astype(jnp.float32), 16, 1)
            packed = jnp.where(lane < 8, high.astype(jnp.float32), jnp.where(lane < 16, mid, low))
            sent_ref[:, width:] = packed.astype(jnp.bfloat16)


def combine_kernel(
    devices, mine, me_ref, lengths_ref, own_ref, level_ref, got_ref, gates_ref, out_ref
):
    rows, width = own_ref.shape
    me = me_ref[0]
    half = place_of(me, devices)[0]
    owner = me if mine else lax.rem(me + devices // 2, devices)
    lane = iota((rows, HEAD_DIM), 1)
    position = iota((rows, HEAD_DIM), 0) + owner * rows
    member = jnp.zeros((rows, HEAD_DIM), jnp.float32)
    for c, (start, end) in enumerate(clip_bounds(lengths_ref)):
        inside = (position >= start) & (position < end)
        member = jnp.where((lane == c) & inside, 1.0, member)
    gates = jnp.where(half == 0, gates_ref[:, :width], gates_ref[:, width:])
    gate = dot(member[:, : gates.shape[0]].astype(jnp.bfloat16), gates)
    stat = got_ref[:, width:].astype(jnp.float32)
    for h in range(width // HEAD_DIM):
        got_level = (stat[:, h : h + 1] + stat[:, h + 8 : h + 9]) + stat[:, h + 16 : h + 17]
        gap = level_ref[:, h : h + 1] - got_level
        own_share = 1.0 / (1.0 + jnp.exp2(-gap))
        got_share = 1.0 / (1.0 + jnp.exp2(gap))
        at = slice(h * HEAD_DIM, (h + 1) * HEAD_DIM)
        mixed = own_ref[:, at] * own_share + got_ref[:, at].astype(jnp.float32) * got_share
        out_ref[:, at] = (mixed * gate[:, at]).astype(jnp.bfloat16)


def join_kernel(devices, me_ref, mine_ref, back_ref, out_ref):
    half = mine_ref.shape[1]
    low, high = slice(0, half), slice(half, 2 * half)
    side = place_of(me_ref[0], devices)[0]

    @pl.when(side == 0)
    def _():
        out_ref[:, low] = mine_ref[...]
        out_ref[:, high] = back_ref[...]

    @pl.when(side != 0)
    def _():
        out_ref[:, low] = back_ref[...]
        out_ref[:, high] = mine_ref[...]


SMEM = pl.BlockSpec(memory_space=pltpu.SMEM)


def whole(shape):
    return pl.BlockSpec(shape, lambda i: (0,) * len(shape))


def attend(dead, queries, blocks, clips, state, last):
    tile, width = queries[0].shape
    heads = width // HEAD_DIM
    sizes = [b.shape[0] for b in blocks]
    keys = sum(sizes)
    rows = 2 * tile
    first = state is None
    operands = [dead, *queries, *blocks, clips] + ([] if first else list(state))
    if last:
        out_shape = [
            jax.ShapeDtypeStruct((tile, width), jnp.float32),
            jax.ShapeDtypeStruct((tile, HEAD_DIM), jnp.float32),
            jax.ShapeDtypeStruct((tile, width + HEAD_DIM), jnp.bfloat16),
        ]
    else:
        out_shape = [
            jax.ShapeDtypeStruct((rows, width), jnp.float32),
            jax.ShapeDtypeStruct((rows, HEAD_DIM), jnp.float32),
        ]
    return pl.pallas_call(
        functools.partial(attend_kernel, sizes, first, last),
        grid=(1,),
        in_specs=[whole(o.shape) for o in operands],
        out_specs=[whole(o.shape) for o in out_shape],
        out_shape=out_shape,
        scratch_shapes=[pltpu.VMEM((2 * heads, tile, keys), jnp.float32)],
        compiler_params=pltpu.CompilerParams(vmem_limit_bytes=ATTEND_VMEM),
        cost_estimate=pl.CostEstimate(
            flops=4 * rows * keys * width,
            bytes_accessed=4 * keys * width,
            transcendentals=rows * keys * heads,
        ),
    )(*operands)


def shards(
    query_rows, key_rows, value_rows, deal_owner, deal_slot, clip_lengths, clip_steps, gate_table
):
    devices = lax.axis_size("seq")
    plane = devices // 2
    ring = plane // 2
    rows, width = query_rows.shape
    half_width = width // 2
    me = lax.axis_index("seq")
    core = me % 2

    def index(h, y, c):
        return h * plane + (y % ring) * 2 + c

    everyone = [(h, y, c) for h in range(2) for y in range(ring) for c in range(2)]
    to_half = [(index(h, y, c), index(1 - h, y, c)) for h, y, c in everyone]
    to_core = [(index(h, y, c), index(h, y, 1 - c)) for h, y, c in everyone]
    to_next = [(index(h, y, c), index(h, y + 1 - 2 * c, c)) for h, y, c in everyone]
    chips = [[2 * i, 2 * i + 1] for i in range(plane)]

    def step(block):
        return lax.ppermute(block, "seq", to_next)

    def chip_gather(block):
        return lax.all_gather(block, "seq", axis_index_groups=chips, tiled=True)

    def core_half(block):
        return lax.dynamic_slice_in_dim(block, core * rows, rows, axis=0)

    def small(kernel, in_specs, outs):
        return pl.pallas_call(
            kernel,
            grid=(1,),
            in_specs=in_specs,
            out_specs=[whole(o.shape) for o in outs],
            out_shape=outs,
            compiler_params=pltpu.CompilerParams(vmem_limit_bytes=SMALL_VMEM),
        )

    def bf16(*shape):
        return jax.ShapeDtypeStruct(shape, jnp.bfloat16)

    def after(value, *others):
        return lax.optimization_barrier((value, *others))[0]

    mine = me[None]
    ring_rows = plane * MSG
    message = pl.pallas_call(
        functools.partial(pack_kernel, plane),
        grid=(1,),
        in_specs=[SMEM, whole((1, rows)), whole((1, rows)), whole((rows, width))],
        out_specs=whole((ring_rows, half_width + HEAD_DIM)),
        out_shape=bf16(ring_rows, half_width + HEAD_DIM),
    )(clip_lengths, deal_owner[None, :], deal_slot[None, :], query_rows)
    got = lax.all_to_all(
        message.reshape(plane, MSG, half_width + HEAD_DIM),
        "seq",
        split_axis=0,
        concat_axis=0,
        axis_index_groups=[list(range(c, devices, 2)) for c in range(2)],
        tiled=True,
    ).reshape(ring_rows, half_width + HEAD_DIM)

    kept, given = pl.pallas_call(
        functools.partial(split_kernel, devices),
        grid=(1,),
        in_specs=[SMEM, whole((rows, width)), whole((rows, width))],
        out_specs=[whole((rows, width))] * 2,
        out_shape=[bf16(rows, width)] * 2,
    )(mine, after(key_rows, message), value_rows)
    taken = lax.ppermute(given, "seq", to_half)
    near0 = chip_gather(kept)
    gates = jnp.take(gate_table, clip_steps, axis=0)
    got, gates = lax.optimization_barrier((got, gates))
    near1 = step(near0)
    near2 = step(near1)
    near3 = step(near2)
    far0 = chip_gather(after(taken, got))
    far1 = step(far0)
    far2 = step(far1)
    early = 10
    *queries, clips0, clips1, dead = small(
        functools.partial(unpack_kernel, devices, early),
        [SMEM, SMEM] + [whole((ring_rows, half_width + HEAD_DIM))] * 2,
        [
            bf16(2 * rows, half_width),
            bf16(2 * rows, half_width),
            bf16(early * rows, HEAD_DIM),
            bf16((plane - early) * rows, HEAD_DIM),
            bf16(4 * rows, HEAD_DIM),
        ],
    )(mine, clip_lengths, got, lax.ppermute(got, "seq", to_core))
    near4 = step(core_half(near3))
    far3 = step(far2)
    far4 = step(core_half(far3))

    state = attend(dead, queries, [kept, taken, near1, near2, far1, near3], clips0, None, False)
    own, level, sent = attend(dead, queries, [far2, far3, near4, far4], clips1, state, True)
    received = lax.ppermute(sent, "seq", to_core)

    def combine(which):
        return small(
            functools.partial(combine_kernel, devices, which == 0),
            [
                SMEM,
                SMEM,
                pl.BlockSpec((rows, half_width), lambda i: (which, 0)),
                pl.BlockSpec((rows, HEAD_DIM), lambda i: (which, 0)),
                pl.BlockSpec((rows, half_width + HEAD_DIM), lambda i: (which, 0)),
                whole(gates.shape),
            ],
            [bf16(rows, half_width)],
        )(mine, clip_lengths, own, level, received, gates)[0]

    back = lax.ppermute(combine(1), "seq", to_half)
    (out,) = small(
        functools.partial(join_kernel, devices),
        [SMEM, whole((rows, half_width)), whole((rows, half_width))],
        [bf16(rows, width)],
    )(mine, combine(0), back)
    return out


def solution(mesh):
    placed = (
        P(("dp", "seq"), "tensor"),
        P(("dp", "seq"), "tensor"),
        P(("dp", "seq"), "tensor"),
        P(("dp", "seq")),
        P(("dp", "seq")),
        P("dp"),
        P("dp"),
        P(None, "tensor"),
    )
    return jax.shard_map(
        shards, mesh=mesh, in_specs=placed, out_specs=P(("dp", "seq"), "tensor"), check_vma=False
    )
```

```python
import functools
import math

import jax
import jax.numpy as jnp
from jax import lax
from jax.experimental import pallas as pl
from jax.experimental.pallas import tpu as pltpu
from jax.sharding import PartitionSpec as P

HEAD_DIM = 128
MASKED = -1e30
SCALE2 = math.log2(math.e) / math.sqrt(HEAD_DIM)
BOUND = 6
MSG = 24
CHUNK = 256
ATTEND_VMEM = 30 * 1024 * 1024
SMALL_VMEM = 10 * 1024 * 1024

NN = (((1,), (0,)), ((), ()))
NT = (((1,), (1,)), ((), ()))
TN = (((0,), (0,)), ((), ()))


def iota(shape, axis):
    return lax.broadcasted_iota(jnp.int32, shape, axis)


def dot(a, b, dims=NN):
    return lax.dot_general(a, b, dims, preferred_element_type=jnp.float32)


def unit(size):
    return (iota((size, size), 0) == iota((size, size), 1)).astype(jnp.bfloat16)


def clip_bounds(lengths_ref):
    bounds = []
    end = jnp.int32(0)
    for c in range(lengths_ref.shape[0]):
        start = end
        end = end + lengths_ref[c]
        bounds.append((start, end))
    return bounds


def split_kernel(devices, me_ref, key_ref, value_ref, kept_ref, given_ref):
    half = key_ref.shape[1] // 2
    low, high = slice(0, half), slice(half, 2 * half)
    side = place_of(me_ref[0], devices)[0]

    @pl.when(side == 0)
    def _():
        kept_ref[:, low] = key_ref[:, low]
        kept_ref[:, high] = value_ref[:, low]
        given_ref[:, low] = key_ref[:, high]
        given_ref[:, high] = value_ref[:, high]

    @pl.when(side != 0)
    def _():
        kept_ref[:, low] = key_ref[:, high]
        kept_ref[:, high] = value_ref[:, high]
        given_ref[:, low] = key_ref[:, low]
        given_ref[:, high] = value_ref[:, low]


def pack_kernel(plane, lengths_ref, owner_ref, slot_ref, query_ref, out_ref):
    rows, width = query_ref.shape
    half = width // 2
    ring = plane // 2
    owner = owner_ref[...]
    slot = slot_ref[...]
    place = owner * rows + slot
    clip = jnp.zeros_like(place)
    for _, end in clip_bounds(lengths_ref):
        clip = clip + (place >= end).astype(jnp.int32)
    clip = jnp.broadcast_to(clip.astype(jnp.float32), (8, rows))
    square = (rows, rows)
    along = jnp.broadcast_to(owner.astype(jnp.float32), square)
    earlier = (along == along.T) & (iota(square, 0) < iota(square, 1))
    rank = jnp.sum(earlier.astype(jnp.float32), axis=0, keepdims=True).astype(jnp.int32)
    there = lax.div(lax.rem(owner, plane), 2)
    which = lax.div(owner, plane) * 2 + lax.rem(owner, 2)
    target = there * MSG + which * BOUND + rank
    spread = (ring * MSG, rows)
    line = iota(spread, 0)
    lane = iota(spread, 1)
    kind = lax.rem(line, MSG)
    pick = (line == target).astype(jnp.bfloat16)
    main = dot(pick, query_ref[...])
    slot_down = jnp.broadcast_to((slot + 1).astype(jnp.float32), square).T
    slots = jnp.where(iota(square, 1) == rows - 1, slot_down, 0.0).astype(jnp.bfloat16)
    meta = dot(pick, slots)
    meta = jnp.where((kind == 0) & (lane < rows // 2), clip[:1], meta)
    turned = pltpu.roll(clip, rows // 2, 1)[:1]
    meta = jnp.where((kind == 1) & (lane < rows // 2), turned, meta).astype(jnp.bfloat16)
    for s in range(2):
        at = slice(s * ring * MSG, (s + 1) * ring * MSG)
        out_ref[at, :half] = main[:, s * half : (s + 1) * half].astype(jnp.bfloat16)
        out_ref[at, half:] = meta


def place_of(me, devices):
    plane = devices // 2
    half = lax.div(me, plane)
    return half, lax.div(lax.rem(me, plane), 2), lax.rem(me, 2)


def key_sources(me, devices):
    plane = devices // 2
    ring = plane // 2
    half, y, core = place_of(me, devices)

    def pair(h, distance):
        there = lax.rem(y + (2 * core - 1) * distance + ring, ring)
        at = h * plane + there * 2
        return [at, at + 1]

    near, far = half, 1 - half
    order = [me, lax.rem(me + plane, devices)]
    for h, distance in ((near, 1), (far, 1), (near, 2), (far, 2), (near, 3), (far, 3)):
        order += pair(h, distance)
    return order + [pair(near, 4)[0] + core, pair(far, 4)[0] + core]


def unpack_kernel(
    devices,
    counts,
    me_ref,
    lengths_ref,
    got_ref,
    other_ref,
    query_ref,
    other_query_ref,
    *refs,
):
    *clip_refs, dead_ref = refs
    each = got_ref.shape[0]
    lines = 2 * each
    rows = HEAD_DIM
    plane = devices // 2
    me = me_ref[0]
    half, _, core = place_of(me, devices)
    got = jnp.concatenate([got_ref[...], other_ref[...]], axis=0)
    data, meta = got[:, :-rows], got[:, -rows:]
    kind = lax.rem(iota((lines, 1), 0), MSG)
    from_half = lax.div(kind, 2 * BOUND)
    from_core = lax.rem(lax.div(kind, BOUND), 2)
    quarter = (from_core != core).astype(jnp.int32) * 2 + (from_half != half).astype(jnp.int32)
    slot = meta[:, rows - 1 :].astype(jnp.float32)
    target = jnp.where(slot > 0, slot - 1.0 + (quarter * rows).astype(jnp.float32), -1.0)
    target = jnp.broadcast_to(target, (lines, rows))
    target = jnp.concatenate(
        [target[i : i + rows, :].T[:1, :] for i in range(0, lines, rows)], axis=1
    )
    put = (iota((4 * rows, lines), 0).astype(jnp.float32) == target).astype(jnp.bfloat16)
    queries = dot(put, data).astype(jnp.bfloat16)
    query_ref[...] = queries[: 2 * rows]
    other_query_ref[...] = queries[2 * rows :]

    order = key_sources(me, devices)
    slots = len(order)
    block = (slots, lines)
    line = iota(block, 0)
    source = jnp.zeros(block, jnp.int32)
    for j, at in enumerate(order):
        at = lax.div(at, 2) * MSG + (lax.rem(at, 2) != core).astype(jnp.int32) * each
        source = jnp.where(line == j, at, source)
    first = dot((source == iota(block, 1)).astype(jnp.bfloat16), meta)
    second = dot((source + 1 == iota(block, 1)).astype(jnp.bfloat16), meta)
    ids = jnp.where(iota((slots, rows), 1) < rows // 2, first, pltpu.roll(second, rows // 2, 1))
    down = iota((rows, rows), 0).astype(jnp.float32)
    for j in range(slots):
        member = (ids[j : j + 1, :] == down).astype(jnp.bfloat16)
        clips = dot(unit(rows), member, NT).astype(jnp.bfloat16)
        call = 0
        while j >= sum(counts[: call + 1]):
            call += 1
        at = (j - sum(counts[:call])) * rows
        clip_refs[call][at : at + rows, :] = clips

    bounds = clip_bounds(lengths_ref)
    other = lax.rem(me + plane, devices)
    away = 1 - 2 * core
    lane = iota((rows, HEAD_DIM), 1)
    for q, owner in enumerate((me, other, me + away, other + away)):
        position = iota((rows, HEAD_DIM), 0) + owner * rows
        dead = jnp.zeros((rows, HEAD_DIM), jnp.float32)
        for c, (start, end) in enumerate(bounds):
            outside = (position < start) | (position >= end)
            dead = jnp.where((lane == c) & outside, MASKED, dead)
        dead_ref[q * rows : (q + 1) * rows, :] = dead.astype(jnp.bfloat16)


def split3(value):
    high = value.astype(jnp.bfloat16)
    rest = value - high.astype(jnp.float32)
    mid = rest.astype(jnp.bfloat16)
    low = (rest - mid.astype(jnp.float32)).astype(jnp.bfloat16)
    return high, mid, low


def pair_up(sizes):
    chunks = []
    at = 0
    parts = []
    for i, size in enumerate(sizes):
        if size >= CHUNK:
            for start in range(0, size, CHUNK):
                chunks.append((at, [(i, start, CHUNK)]))
                at += CHUNK
            continue
        parts.append((i, 0, size))
        if sum(p[2] for p in parts) == CHUNK:
            chunks.append((at, parts))
            at += CHUNK
            parts = []
    assert not parts
    return chunks


def attend_kernel(sizes, first, last, *refs):
    refs = list(refs)
    dead_ref = refs.pop(0)
    query_refs = [refs.pop(0), refs.pop(0)]
    block_refs = [refs.pop(0) for _ in sizes]
    clip_ref = refs.pop(0)
    if not first:
        sum_ref, stat_ref = refs.pop(0), refs.pop(0)
    if last:
        out_ref, level_ref, sent_ref = refs.pop(0), refs.pop(0), refs.pop(0)
    else:
        new_sum_ref, new_stat_ref = refs.pop(0), refs.pop(0)
    scores = refs.pop(0)
    tile, width = query_refs[0].shape
    heads = width // HEAD_DIM
    lane = iota((tile, HEAD_DIM), 1)
    chunks = pair_up(sizes)
    ones = jnp.ones((CHUNK, HEAD_DIM), jnp.bfloat16)
    for t in range(2):
        rows = slice(t * tile, (t + 1) * tile)
        stat = jnp.zeros((tile, HEAD_DIM), jnp.float32)
        for h in range(heads):
            key_at = slice(h * HEAD_DIM, (h + 1) * HEAD_DIM)
            value_at = slice(width + h * HEAD_DIM, width + (h + 1) * HEAD_DIM)
            query = jnp.concatenate([query_refs[t][:, key_at], dead_ref[rows, :]], axis=1)
            top = jnp.full((tile, HEAD_DIM), -3e38, jnp.float32)
            for at, members in chunks:
                key = jnp.concatenate([block_refs[i][o : o + n, key_at] for i, o, n in members])
                key = jnp.concatenate([key, clip_ref[at : at + CHUNK, :]], axis=1)
                s = dot(query, key, NT)
                scores[t * heads + h, :, at : at + CHUNK] = s
                for j in range(0, CHUNK, HEAD_DIM):
                    top = jnp.maximum(top, s[:, j : j + HEAD_DIM])
            top = jnp.max(top, axis=1, keepdims=True) * SCALE2
            if first:
                total = jnp.zeros((tile, 2 * HEAD_DIM), jnp.float32)
            else:
                old_top = stat_ref[rows, h : h + 1]
                top = jnp.maximum(top, old_top)
                fade = jnp.exp2(old_top - top)
                weight = stat_ref[rows, h + 8 : h + 9] * fade
                weight = jnp.broadcast_to(weight, (tile, HEAD_DIM))
                total = jnp.concatenate([sum_ref[rows, key_at] * fade, weight], axis=1)
            for at, members in chunks:
                w = scores[t * heads + h, :, at : at + CHUNK] * SCALE2 - top
                w = jnp.exp2(w).astype(jnp.bfloat16)
                value = jnp.concatenate([block_refs[i][o : o + n, value_at] for i, o, n in members])
                total = total + dot(w, jnp.concatenate([value, ones], axis=1))
            weight = total[:, HEAD_DIM:]
            if not last:
                new_sum_ref[rows, key_at] = total[:, :HEAD_DIM]
                stat = jnp.where(lane == h, top, stat)
                stat = jnp.where(lane == h + 8, weight, stat)
                continue
            out = total[:, :HEAD_DIM] / weight
            stat = jnp.where(lane == h, top + jnp.log2(weight), stat)
            if t == 0:
                out_ref[:, key_at] = out
            else:
                sent_ref[:, key_at] = out.astype(jnp.bfloat16)
        if not last:
            new_stat_ref[rows, :] = stat
        elif t == 0:
            level_ref[...] = stat
        else:
            high, mid, low = split3(stat)
            mid = pltpu.roll(mid.astype(jnp.float32), 8, 1)
            low = pltpu.roll(low.astype(jnp.float32), 16, 1)
            packed = jnp.where(lane < 8, high.astype(jnp.float32), jnp.where(lane < 16, mid, low))
            sent_ref[:, width:] = packed.astype(jnp.bfloat16)


def combine_kernel(
    devices, which, me_ref, lengths_ref, own_ref, level_ref, got_ref, gates_ref, out_ref
):
    rows, width = own_ref.shape
    me = me_ref[0]
    half, _, core = place_of(me, devices)
    owner = lax.rem(me + which * (devices // 2), devices)
    other = pl.multiple_of((1 - core) * 2 * rows + which * rows, rows)
    got = got_ref[pl.ds(other, rows), :]
    lane = iota((rows, HEAD_DIM), 1)
    position = iota((rows, HEAD_DIM), 0) + owner * rows
    member = jnp.zeros((rows, HEAD_DIM), jnp.float32)
    for c, (start, end) in enumerate(clip_bounds(lengths_ref)):
        inside = (position >= start) & (position < end)
        member = jnp.where((lane == c) & inside, 1.0, member)
    gates = jnp.where(half == 0, gates_ref[:, :width], gates_ref[:, width:])
    gate = dot(member[:, : gates.shape[0]].astype(jnp.bfloat16), gates)
    stat = got[:, width:].astype(jnp.float32)
    for h in range(width // HEAD_DIM):
        got_level = (stat[:, h : h + 1] + stat[:, h + 8 : h + 9]) + stat[:, h + 16 : h + 17]
        gap = level_ref[:, h : h + 1] - got_level
        own_share = 1.0 / (1.0 + jnp.exp2(-gap))
        got_share = 1.0 / (1.0 + jnp.exp2(gap))
        at = slice(h * HEAD_DIM, (h + 1) * HEAD_DIM)
        mixed = own_ref[:, at] * own_share + got[:, at].astype(jnp.float32) * got_share
        out_ref[:, at] = (mixed * gate[:, at]).astype(jnp.bfloat16)


def join_kernel(devices, me_ref, mine_ref, back_ref, out_ref):
    half = mine_ref.shape[1]
    low, high = slice(0, half), slice(half, 2 * half)
    side = place_of(me_ref[0], devices)[0]

    @pl.when(side == 0)
    def _():
        out_ref[:, low] = mine_ref[...]
        out_ref[:, high] = back_ref[...]

    @pl.when(side != 0)
    def _():
        out_ref[:, low] = back_ref[...]
        out_ref[:, high] = mine_ref[...]


SMEM = pl.BlockSpec(memory_space=pltpu.SMEM)


def whole(shape):
    return pl.BlockSpec(shape, lambda i: (0,) * len(shape))


def call(kernel, operands, in_specs, outs, behind=(), scratch=(), vmem=None, token=False):
    taken, extra = len(operands), len(behind)

    def body(*refs):
        ins, rest = refs[:taken], list(refs[taken + extra :])
        if token:
            done = rest.pop(len(outs))
            done[...] = jnp.zeros(done.shape, done.dtype)
        kernel(*ins, *rest)

    results = list(outs) + ([jax.ShapeDtypeStruct((8, HEAD_DIM), jnp.float32)] if token else [])
    return pl.pallas_call(
        body,
        grid=(1,),
        in_specs=list(in_specs) + [pl.BlockSpec(memory_space=pl.ANY)] * extra,
        out_specs=[whole(o.shape) for o in results],
        out_shape=results,
        scratch_shapes=scratch,
        compiler_params=pltpu.CompilerParams(vmem_limit_bytes=vmem),
        cost_estimate=pl.CostEstimate(flops=0, bytes_accessed=0, transcendentals=0),
    )(*operands, *behind)


def attend(dead, queries, blocks, clips, state, last, token=False, behind=()):
    tile, width = queries[0].shape
    heads = width // HEAD_DIM
    sizes = [b.shape[0] for b in blocks]
    keys = sum(sizes)
    rows = 2 * tile
    first = state is None
    operands = [dead, *queries, *blocks, clips] + ([] if first else list(state))
    if last:
        outs = [
            jax.ShapeDtypeStruct((tile, width), jnp.float32),
            jax.ShapeDtypeStruct((tile, HEAD_DIM), jnp.float32),
            jax.ShapeDtypeStruct((tile, width + HEAD_DIM), jnp.bfloat16),
        ]
    else:
        outs = [
            jax.ShapeDtypeStruct((rows, width), jnp.float32),
            jax.ShapeDtypeStruct((rows, HEAD_DIM), jnp.float32),
        ]
    return call(
        functools.partial(attend_kernel, sizes, first, last),
        operands,
        [whole(o.shape) for o in operands],
        outs,
        behind,
        [pltpu.VMEM((2 * heads, tile, keys), jnp.float32)],
        ATTEND_VMEM,
        token,
    )


def shards(
    query_rows, key_rows, value_rows, deal_owner, deal_slot, clip_lengths, clip_steps, gate_table
):
    devices = lax.axis_size("seq")
    plane = devices // 2
    ring = plane // 2
    rows, width = query_rows.shape
    half_width = width // 2
    me = lax.axis_index("seq")
    core = me % 2

    def index(h, y, c):
        return h * plane + (y % ring) * 2 + c

    everyone = [(h, y, c) for h in range(2) for y in range(ring) for c in range(2)]
    to_half = [(index(h, y, c), index(1 - h, y, c)) for h, y, c in everyone]
    to_core = [(index(h, y, c), index(h, y, 1 - c)) for h, y, c in everyone]
    to_next = [(index(h, y, c), index(h, y + 1 - 2 * c, c)) for h, y, c in everyone]
    chips = [[2 * i, 2 * i + 1] for i in range(plane)]

    def step(block):
        return lax.ppermute(block, "seq", to_next)

    def chip_gather(block):
        return lax.all_gather(block, "seq", axis_index_groups=chips, tiled=True)

    def core_half(block):
        return lax.dynamic_slice_in_dim(block, core * rows, rows, axis=0)

    def bf16(*shape):
        return jax.ShapeDtypeStruct(shape, jnp.bfloat16)

    mine = me[None]
    sent_rows = plane * MSG
    sent_width = half_width + HEAD_DIM
    kept, given = call(
        functools.partial(split_kernel, devices),
        [mine, key_rows, value_rows],
        [SMEM, whole((rows, width)), whole((rows, width))],
        [bf16(rows, width)] * 2,
    )
    taken = lax.ppermute(given, "seq", to_half)
    near0 = chip_gather(kept)
    (message,) = call(
        functools.partial(pack_kernel, plane),
        [clip_lengths, deal_owner[None, :], deal_slot[None, :], query_rows],
        [SMEM, whole((1, rows)), whole((1, rows)), whole((rows, width))],
        [bf16(sent_rows, sent_width)],
        [near0],
    )
    got = lax.all_to_all(
        message.reshape(plane, MSG, sent_width),
        "seq",
        split_axis=0,
        concat_axis=0,
        axis_index_groups=[list(range(c, devices, 2)) for c in range(2)],
        tiled=True,
    ).reshape(sent_rows, sent_width)

    near1 = step(near0)
    far1 = step(chip_gather(taken))
    near2 = step(near1)
    far2 = step(far1)
    near2, got = lax.optimization_barrier((near2, got))
    near3 = step(near2)
    far3 = step(far2)
    near4 = step(core_half(near3))
    gates = jnp.take(gate_table, clip_steps, axis=0)
    counts = (12, 4)
    *queries, clips0, clips1, dead, unpacked = call(
        functools.partial(unpack_kernel, devices, counts),
        [mine, clip_lengths, got, lax.ppermute(got, "seq", to_core)],
        [SMEM, SMEM] + [whole((sent_rows, sent_width))] * 2,
        [bf16(2 * rows, half_width)] * 2
        + [bf16(c * rows, HEAD_DIM) for c in counts]
        + [bf16(4 * rows, HEAD_DIM)],
        [gates],
        vmem=SMALL_VMEM,
        token=True,
    )
    half3, unpacked = lax.optimization_barrier((core_half(far3), unpacked))
    far4 = step(half3)
    blocks = [kept, taken, near1, far1, near2, far2, near3]
    state = attend(dead, queries, blocks, clips0, None, False)
    own, level, sent = attend(
        dead, queries, [far3, near4, far4], clips1, state, True, behind=[unpacked]
    )
    received = chip_gather(sent)

    def combine(which):
        return call(
            functools.partial(combine_kernel, devices, which),
            [mine, clip_lengths, own, level, received, gates],
            [
                SMEM,
                SMEM,
                pl.BlockSpec((rows, half_width), lambda i: (which, 0)),
                pl.BlockSpec((rows, HEAD_DIM), lambda i: (which, 0)),
                whole((4 * rows, sent_width)),
                whole(gates.shape),
            ],
            [bf16(rows, half_width)],
            vmem=SMALL_VMEM,
        )[0]

    back = lax.ppermute(combine(1), "seq", to_half)
    return call(
        functools.partial(join_kernel, devices),
        [mine, combine(0), back],
        [SMEM, whole((rows, half_width)), whole((rows, half_width))],
        [bf16(rows, width)],
        vmem=SMALL_VMEM,
    )[0]


def solution(mesh):
    placed = (
        P(("dp", "seq"), "tensor"),
        P(("dp", "seq"), "tensor"),
        P(("dp", "seq"), "tensor"),
        P(("dp", "seq")),
        P(("dp", "seq")),
        P("dp"),
        P("dp"),
        P(None, "tensor"),
    )
    return jax.shard_map(
        shards, mesh=mesh, in_specs=placed, out_specs=P(("dp", "seq"), "tensor"), check_vma=False
    )
```

```python
import functools
import math

import jax
import jax.numpy as jnp
from jax import lax
from jax.experimental import pallas as pl
from jax.experimental.pallas import tpu as pltpu
from jax.sharding import PartitionSpec as P

HEAD_DIM = 128
MASKED = -1e30
SCALE2 = math.log2(math.e) / math.sqrt(HEAD_DIM)
BOUND = 6
MSG = 24
CHUNK = 256
ATTEND_VMEM = 30 * 1024 * 1024
SMALL_VMEM = 10 * 1024 * 1024

NN = (((1,), (0,)), ((), ()))
NT = (((1,), (1,)), ((), ()))
TN = (((0,), (0,)), ((), ()))


def iota(shape, axis):
    return lax.broadcasted_iota(jnp.int32, shape, axis)


def dot(a, b, dims=NN):
    return lax.dot_general(a, b, dims, preferred_element_type=jnp.float32)


def unit(size):
    return (iota((size, size), 0) == iota((size, size), 1)).astype(jnp.bfloat16)


def clip_bounds(lengths_ref):
    bounds = []
    end = jnp.int32(0)
    for c in range(lengths_ref.shape[0]):
        start = end
        end = end + lengths_ref[c]
        bounds.append((start, end))
    return bounds


def split_kernel(devices, me_ref, key_ref, value_ref, kept_ref, given_ref):
    half = key_ref.shape[1] // 2
    low, high = slice(0, half), slice(half, 2 * half)
    side = place_of(me_ref[0], devices)[0]

    @pl.when(side == 0)
    def _():
        kept_ref[:, low] = key_ref[:, low]
        kept_ref[:, high] = value_ref[:, low]
        given_ref[:, low] = key_ref[:, high]
        given_ref[:, high] = value_ref[:, high]

    @pl.when(side != 0)
    def _():
        kept_ref[:, low] = key_ref[:, high]
        kept_ref[:, high] = value_ref[:, high]
        given_ref[:, low] = key_ref[:, low]
        given_ref[:, high] = value_ref[:, low]


def pack_kernel(plane, lengths_ref, owner_ref, slot_ref, query_ref, out_ref):
    rows, width = query_ref.shape
    half = width // 2
    ring = plane // 2
    owner = owner_ref[...]
    slot = slot_ref[...]
    place = owner * rows + slot
    clip = jnp.zeros_like(place)
    for _, end in clip_bounds(lengths_ref):
        clip = clip + (place >= end).astype(jnp.int32)
    clip = jnp.broadcast_to(clip.astype(jnp.float32), (8, rows))
    square = (rows, rows)
    along = jnp.broadcast_to(owner.astype(jnp.float32), square)
    earlier = (along == along.T) & (iota(square, 0) < iota(square, 1))
    rank = jnp.sum(earlier.astype(jnp.float32), axis=0, keepdims=True).astype(jnp.int32)
    there = lax.div(lax.rem(owner, plane), 2)
    which = lax.div(owner, plane) * 2 + lax.rem(owner, 2)
    target = there * MSG + which * BOUND + rank
    spread = (ring * MSG, rows)
    line = iota(spread, 0)
    lane = iota(spread, 1)
    kind = lax.rem(line, MSG)
    pick = (line == target).astype(jnp.bfloat16)
    main = dot(pick, query_ref[...])
    slot_down = jnp.broadcast_to((slot + 1).astype(jnp.float32), square).T
    slots = jnp.where(iota(square, 1) == rows - 1, slot_down, 0.0).astype(jnp.bfloat16)
    meta = dot(pick, slots)
    meta = jnp.where((kind == 0) & (lane < rows // 2), clip[:1], meta)
    turned = pltpu.roll(clip, rows // 2, 1)[:1]
    meta = jnp.where((kind == 1) & (lane < rows // 2), turned, meta).astype(jnp.bfloat16)
    for s in range(2):
        at = slice(s * ring * MSG, (s + 1) * ring * MSG)
        out_ref[at, :half] = main[:, s * half : (s + 1) * half].astype(jnp.bfloat16)
        out_ref[at, half:] = meta


def place_of(me, devices):
    plane = devices // 2
    half = lax.div(me, plane)
    return half, lax.div(lax.rem(me, plane), 2), lax.rem(me, 2)


def key_sources(me, devices):
    plane = devices // 2
    ring = plane // 2
    half, y, core = place_of(me, devices)

    def pair(h, distance):
        there = lax.rem(y + (2 * core - 1) * distance + ring, ring)
        at = h * plane + there * 2
        return [at, at + 1]

    near, far = half, 1 - half
    order = [me, lax.rem(me + plane, devices)]
    for h, distance in ((near, 1), (far, 1), (near, 2), (far, 2), (near, 3), (far, 3)):
        order += pair(h, distance)
    return order + [pair(near, 4)[0] + core, pair(far, 4)[0] + core]


def unpack_kernel(
    devices,
    counts,
    me_ref,
    lengths_ref,
    got_ref,
    other_ref,
    far_query_ref,
    near_query_ref,
    *refs,
):
    *clip_refs, dead_ref = refs
    each = got_ref.shape[0]
    lines = 2 * each
    rows = HEAD_DIM
    plane = devices // 2
    me = me_ref[0]
    half, _, core = place_of(me, devices)
    got = jnp.concatenate([got_ref[...], other_ref[...]], axis=0)
    data, meta = got[:, :-rows], got[:, -rows:]
    kind = lax.rem(iota((lines, 1), 0), MSG)
    from_half = lax.div(kind, 2 * BOUND)
    from_core = lax.rem(lax.div(kind, BOUND), 2)
    quarter = (from_half == half).astype(jnp.int32) * 2 + (from_core != core).astype(jnp.int32)
    slot = meta[:, rows - 1 :].astype(jnp.float32)
    target = jnp.where(slot > 0, slot - 1.0 + (quarter * rows).astype(jnp.float32), -1.0)
    target = jnp.broadcast_to(target, (lines, rows))
    target = jnp.concatenate(
        [target[i : i + rows, :].T[:1, :] for i in range(0, lines, rows)], axis=1
    )
    put = (iota((4 * rows, lines), 0).astype(jnp.float32) == target).astype(jnp.bfloat16)
    queries = dot(put, data).astype(jnp.bfloat16)
    far_query_ref[...] = queries[: 2 * rows]
    near_query_ref[...] = queries[2 * rows :]

    order = key_sources(me, devices)
    slots = len(order)
    block = (slots, lines)
    line = iota(block, 0)
    source = jnp.zeros(block, jnp.int32)
    for j, at in enumerate(order):
        at = lax.div(at, 2) * MSG + (lax.rem(at, 2) != core).astype(jnp.int32) * each
        source = jnp.where(line == j, at, source)
    first = dot((source == iota(block, 1)).astype(jnp.bfloat16), meta)
    second = dot((source + 1 == iota(block, 1)).astype(jnp.bfloat16), meta)
    ids = jnp.where(iota((slots, rows), 1) < rows // 2, first, pltpu.roll(second, rows // 2, 1))
    down = iota((rows, rows), 0).astype(jnp.float32)
    for j in range(slots):
        member = (ids[j : j + 1, :] == down).astype(jnp.bfloat16)
        clips = dot(unit(rows), member, NT).astype(jnp.bfloat16)
        call = 0
        while j >= sum(counts[: call + 1]):
            call += 1
        at = (j - sum(counts[:call])) * rows
        clip_refs[call][at : at + rows, :] = clips

    bounds = clip_bounds(lengths_ref)
    other = lax.rem(me + plane, devices)
    away = 1 - 2 * core
    lane = iota((rows, HEAD_DIM), 1)
    for q, owner in enumerate((other, other + away, me, me + away)):
        position = iota((rows, HEAD_DIM), 0) + owner * rows
        dead = jnp.zeros((rows, HEAD_DIM), jnp.float32)
        for c, (start, end) in enumerate(bounds):
            outside = (position < start) | (position >= end)
            dead = jnp.where((lane == c) & outside, MASKED, dead)
        dead_ref[q * rows : (q + 1) * rows, :] = dead.astype(jnp.bfloat16)


def split3(value):
    high = value.astype(jnp.bfloat16)
    rest = value - high.astype(jnp.float32)
    mid = rest.astype(jnp.bfloat16)
    low = (rest - mid.astype(jnp.float32)).astype(jnp.bfloat16)
    return high, mid, low


def pair_up(sizes):
    chunks = []
    at = 0
    parts = []
    for i, size in enumerate(sizes):
        if size >= CHUNK:
            for start in range(0, size, CHUNK):
                chunks.append((at, [(i, start, CHUNK)]))
                at += CHUNK
            continue
        parts.append((i, 0, size))
        if sum(p[2] for p in parts) == CHUNK:
            chunks.append((at, parts))
            at += CHUNK
            parts = []
    assert not parts
    return chunks


def attend_kernel(tiles, sizes, first, last, *refs):
    refs = list(refs)
    dead_ref = refs.pop(0)
    query_refs = [refs.pop(0) for _ in range(tiles)]
    block_refs = [refs.pop(0) for _ in sizes]
    clip_ref = refs.pop(0)
    if not first:
        sum_ref, stat_ref = refs.pop(0), refs.pop(0)
    if last:
        out_ref, level_ref, sent_ref = refs.pop(0), refs.pop(0), refs.pop(0)
    else:
        new_sum_ref, new_stat_ref = refs.pop(0), refs.pop(0)
    scores = refs.pop(0)
    tile, width = query_refs[0].shape
    heads = width // HEAD_DIM
    lane = iota((tile, HEAD_DIM), 1)
    chunks = pair_up(sizes)
    ones = jnp.ones((CHUNK, HEAD_DIM), jnp.bfloat16)
    stats = [jnp.zeros((tile, HEAD_DIM), jnp.float32) for _ in range(tiles)]

    def columns(h):
        return slice(h * HEAD_DIM, (h + 1) * HEAD_DIM)

    def score(t, h):
        rows = slice(t * tile, (t + 1) * tile)
        query = jnp.concatenate([query_refs[t][:, columns(h)], dead_ref[rows, :]], axis=1)
        top = jnp.full((tile, HEAD_DIM), -3e38, jnp.float32)
        for at, members in chunks:
            key = jnp.concatenate([block_refs[i][o : o + n, columns(h)] for i, o, n in members])
            key = jnp.concatenate([key, clip_ref[at : at + CHUNK, :]], axis=1)
            s = dot(query, key, NT)
            scores[t * heads + h, :, at : at + CHUNK] = s
            for j in range(0, CHUNK, HEAD_DIM):
                top = jnp.maximum(top, s[:, j : j + HEAD_DIM])
        return top

    def finish(t, h, top):
        rows = slice(t * tile, (t + 1) * tile)
        top = jnp.max(top, axis=1, keepdims=True) * SCALE2
        if first:
            total = jnp.zeros((tile, 2 * HEAD_DIM), jnp.float32)
        else:
            old_top = stat_ref[rows, h : h + 1]
            top = jnp.maximum(top, old_top)
            fade = jnp.exp2(old_top - top)
            weight = stat_ref[rows, h + 8 : h + 9] * fade
            weight = jnp.broadcast_to(weight, (tile, HEAD_DIM))
            total = jnp.concatenate([sum_ref[rows, columns(h)] * fade, weight], axis=1)
        for at, members in chunks:
            w = scores[t * heads + h, :, at : at + CHUNK] * SCALE2 - top
            w = jnp.exp2(w).astype(jnp.bfloat16)
            value = jnp.concatenate(
                [block_refs[i][o : o + n, columns(heads + h)] for i, o, n in members]
            )
            total = total + dot(w, jnp.concatenate([value, ones], axis=1))
        weight = total[:, HEAD_DIM:]
        if not last:
            new_sum_ref[rows, columns(h)] = total[:, :HEAD_DIM]
            stats[t] = jnp.where(lane == h, top, stats[t])
            stats[t] = jnp.where(lane == h + 8, weight, stats[t])
            return
        out = total[:, :HEAD_DIM] / weight
        stats[t] = jnp.where(lane == h, top + jnp.log2(weight), stats[t])
        out_ref[:, columns(h)] = out[: tile // 2]
        sent_ref[:, columns(h)] = out[tile // 2 :].astype(jnp.bfloat16)

    jobs = [(t, h) for t in range(tiles) for h in range(heads)]
    ahead = score(*jobs[0])
    for n, job in enumerate(jobs):
        top = ahead
        if n + 1 < len(jobs):
            ahead = score(*jobs[n + 1])
        finish(*job, top)
    if not last:
        for t in range(tiles):
            new_stat_ref[t * tile : (t + 1) * tile, :] = stats[t]
        return
    level_ref[...] = stats[0][: tile // 2]
    lane = lane[tile // 2 :]
    high, mid, low = split3(stats[0][tile // 2 :])
    mid = pltpu.roll(mid.astype(jnp.float32), 8, 1)
    low = pltpu.roll(low.astype(jnp.float32), 16, 1)
    packed = jnp.where(lane < 8, high.astype(jnp.float32), jnp.where(lane < 16, mid, low))
    sent_ref[:, width:] = packed.astype(jnp.bfloat16)


def combine_kernel(
    devices, which, me_ref, lengths_ref, own_ref, level_ref, got_ref, gates_ref, out_ref
):
    rows, width = own_ref.shape
    me = me_ref[0]
    half, _, core = place_of(me, devices)
    owner = lax.rem(me + (1 - which) * (devices // 2), devices)
    other = pl.multiple_of((1 - core) * rows, rows)
    got = got_ref[pl.ds(other, rows), :]
    lane = iota((rows, HEAD_DIM), 1)
    position = iota((rows, HEAD_DIM), 0) + owner * rows
    member = jnp.zeros((rows, HEAD_DIM), jnp.float32)
    for c, (start, end) in enumerate(clip_bounds(lengths_ref)):
        inside = (position >= start) & (position < end)
        member = jnp.where((lane == c) & inside, 1.0, member)
    gates = jnp.where(half == 0, gates_ref[:, :width], gates_ref[:, width:])
    gate = dot(member[:, : gates.shape[0]].astype(jnp.bfloat16), gates)
    stat = got[:, width:].astype(jnp.float32)
    for h in range(width // HEAD_DIM):
        got_level = (stat[:, h : h + 1] + stat[:, h + 8 : h + 9]) + stat[:, h + 16 : h + 17]
        gap = level_ref[:, h : h + 1] - got_level
        own_share = 1.0 / (1.0 + jnp.exp2(-gap))
        got_share = 1.0 / (1.0 + jnp.exp2(gap))
        at = slice(h * HEAD_DIM, (h + 1) * HEAD_DIM)
        mixed = own_ref[:, at] * own_share + got[:, at].astype(jnp.float32) * got_share
        out_ref[:, at] = (mixed * gate[:, at]).astype(jnp.bfloat16)


def join_kernel(devices, me_ref, mine_ref, back_ref, out_ref):
    half = mine_ref.shape[1]
    low, high = slice(0, half), slice(half, 2 * half)
    side = place_of(me_ref[0], devices)[0]

    @pl.when(side == 0)
    def _():
        out_ref[:, low] = mine_ref[...]
        out_ref[:, high] = back_ref[...]

    @pl.when(side != 0)
    def _():
        out_ref[:, low] = back_ref[...]
        out_ref[:, high] = mine_ref[...]


SMEM = pl.BlockSpec(memory_space=pltpu.SMEM)


def whole(shape):
    return pl.BlockSpec(shape, lambda i: (0,) * len(shape))


def call(kernel, operands, in_specs, outs, behind=(), scratch=(), vmem=None, token=False, cost=0):
    taken, extra = len(operands), len(behind)

    def body(*refs):
        ins, rest = refs[:taken], list(refs[taken + extra :])
        if token:
            done = rest.pop(len(outs))
            done[...] = jnp.zeros(done.shape, done.dtype)
        kernel(*ins, *rest)

    results = list(outs) + ([jax.ShapeDtypeStruct((8, HEAD_DIM), jnp.float32)] if token else [])
    return pl.pallas_call(
        body,
        grid=(1,),
        in_specs=list(in_specs) + [pl.BlockSpec(memory_space=pl.ANY)] * extra,
        out_specs=[whole(o.shape) for o in results],
        out_shape=results,
        scratch_shapes=scratch,
        compiler_params=pltpu.CompilerParams(vmem_limit_bytes=vmem),
        cost_estimate=pl.CostEstimate(flops=0, bytes_accessed=cost, transcendentals=0),
    )(*operands, *behind)


def attend(dead, queries, blocks, clips, behind=()):
    tile, width = queries[0].shape
    sizes = [b.shape[0] for b in blocks]
    rows = 2 * tile
    operands = [dead, *queries, *blocks, clips]
    return call(
        functools.partial(attend_kernel, 2, sizes, True, False),
        operands,
        [whole(o.shape) for o in operands],
        [
            jax.ShapeDtypeStruct((rows, width), jnp.float32),
            jax.ShapeDtypeStruct((rows, HEAD_DIM), jnp.float32),
        ],
        behind,
        [pltpu.VMEM((2 * width // HEAD_DIM, tile, sum(sizes)), jnp.float32)],
        ATTEND_VMEM,
    )


def attend_last(which, dead, queries, blocks, clips, state, behind=()):
    query = queries[which]
    tile, width = query.shape
    sizes = [b.shape[0] for b in blocks]

    def part(array):
        return pl.BlockSpec((tile, array.shape[1]), lambda i: (which, 0))

    return call(
        functools.partial(attend_kernel, 1, sizes, False, True),
        [dead, query, *blocks, clips, *state],
        [part(dead), whole(query.shape)]
        + [whole(b.shape) for b in blocks]
        + [whole(clips.shape)]
        + [part(s) for s in state],
        [
            jax.ShapeDtypeStruct((tile // 2, width), jnp.float32),
            jax.ShapeDtypeStruct((tile // 2, HEAD_DIM), jnp.float32),
            jax.ShapeDtypeStruct((tile // 2, width + HEAD_DIM), jnp.bfloat16),
        ],
        behind,
        [pltpu.VMEM((width // HEAD_DIM, tile, sum(sizes)), jnp.float32)],
        ATTEND_VMEM,
    )


def shards(
    query_rows, key_rows, value_rows, deal_owner, deal_slot, clip_lengths, clip_steps, gate_table
):
    devices = lax.axis_size("seq")
    plane = devices // 2
    ring = plane // 2
    rows, width = query_rows.shape
    half_width = width // 2
    me = lax.axis_index("seq")
    core = me % 2

    def index(h, y, c):
        return h * plane + (y % ring) * 2 + c

    everyone = [(h, y, c) for h in range(2) for y in range(ring) for c in range(2)]
    to_half = [(index(h, y, c), index(1 - h, y, c)) for h, y, c in everyone]
    to_core = [(index(h, y, c), index(h, y, 1 - c)) for h, y, c in everyone]
    to_next = [(index(h, y, c), index(h, y + 1 - 2 * c, c)) for h, y, c in everyone]
    to_second = [(index(h, y, c), index(h, y + 2 - 4 * c, c)) for h, y, c in everyone]
    chips = [[2 * i, 2 * i + 1] for i in range(plane)]

    def step(block):
        return lax.ppermute(block, "seq", to_next)

    def chip_gather(block):
        return lax.all_gather(block, "seq", axis_index_groups=chips, tiled=True)

    def core_half(block):
        return lax.dynamic_slice_in_dim(block, core * rows, rows, axis=0)

    def bf16(*shape):
        return jax.ShapeDtypeStruct(shape, jnp.bfloat16)

    mine = me[None]
    sent_rows = plane * MSG
    sent_width = half_width + HEAD_DIM
    kept, given = call(
        functools.partial(split_kernel, devices),
        [mine, key_rows, value_rows],
        [SMEM, whole((rows, width)), whole((rows, width))],
        [bf16(rows, width)] * 2,
    )
    taken = lax.ppermute(given, "seq", to_half)
    (message,) = call(
        functools.partial(pack_kernel, plane),
        [clip_lengths, deal_owner[None, :], deal_slot[None, :], query_rows],
        [SMEM, whole((1, rows)), whole((1, rows)), whole((rows, width))],
        [bf16(sent_rows, sent_width)],
        [given],
        cost=8 * 1024 * 1024,
    )
    kept, message = lax.optimization_barrier((kept, message))
    near0 = chip_gather(kept)
    got = lax.all_to_all(
        message.reshape(plane, MSG, sent_width),
        "seq",
        split_axis=0,
        concat_axis=0,
        axis_index_groups=[list(range(c, devices, 2)) for c in range(2)],
        tiled=True,
    ).reshape(sent_rows, sent_width)

    near1 = step(near0)
    far1 = step(chip_gather(taken))
    near2 = step(near1)
    far2 = step(far1)
    near2, got = lax.optimization_barrier((near2, got))
    near3 = step(near2)
    far3 = step(far2)
    near4 = step(core_half(near3))
    gates = jnp.take(gate_table, clip_steps, axis=0)
    counts = (12, 4)
    *queries, clips0, clips1, dead = call(
        functools.partial(unpack_kernel, devices, counts),
        [mine, clip_lengths, got, lax.ppermute(got, "seq", to_core)],
        [SMEM, SMEM] + [whole((sent_rows, sent_width))] * 2,
        [bf16(2 * rows, half_width)] * 2
        + [bf16(c * rows, HEAD_DIM) for c in counts]
        + [bf16(4 * rows, HEAD_DIM)],
        [gates],
        vmem=SMALL_VMEM,
    )
    far4 = lax.ppermute(core_half(far2), "seq", to_second)
    blocks = [kept, taken, near1, far1, near2, far2, near3]
    state = attend(dead, queries, blocks, clips0)

    def finish(which, behind):
        own, level, sent = attend_last(
            which, dead, queries, [far3, near4, far4], clips1, state, behind
        )
        operands = [mine, clip_lengths, own, level, chip_gather(sent), gates]
        return call(
            functools.partial(combine_kernel, devices, which),
            operands,
            [SMEM, SMEM] + [whole(o.shape) for o in operands[2:]],
            [bf16(rows, half_width)],
            vmem=SMALL_VMEM,
        )[0]

    theirs = finish(0, [])
    back = lax.ppermute(theirs, "seq", to_half)
    ours = finish(1, [theirs])
    return call(
        functools.partial(join_kernel, devices),
        [mine, ours, back],
        [SMEM, whole((rows, half_width)), whole((rows, half_width))],
        [bf16(rows, width)],
        vmem=SMALL_VMEM,
    )[0]


def solution(mesh):
    placed = (
        P(("dp", "seq"), "tensor"),
        P(("dp", "seq"), "tensor"),
        P(("dp", "seq"), "tensor"),
        P(("dp", "seq")),
        P(("dp", "seq")),
        P("dp"),
        P("dp"),
        P(None, "tensor"),
    )
    return jax.shard_map(
        shards, mesh=mesh, in_specs=placed, out_specs=P(("dp", "seq"), "tensor"), check_vma=False
    )
```

```python
import functools
import math

import jax
import jax.numpy as jnp
from jax import lax
from jax.experimental import pallas as pl
from jax.experimental.pallas import tpu as pltpu
from jax.sharding import PartitionSpec as P

HEAD_DIM = 128
MASKED = -1e30
SCALE2 = math.log2(math.e) / math.sqrt(HEAD_DIM)
BOUND = 6
MSG = 24
CHUNK = 256
ATTEND_VMEM = 30 * 1024 * 1024
SMALL_VMEM = 10 * 1024 * 1024

NN = (((1,), (0,)), ((), ()))
NT = (((1,), (1,)), ((), ()))
TN = (((0,), (0,)), ((), ()))


def iota(shape, axis):
    return lax.broadcasted_iota(jnp.int32, shape, axis)


def dot(a, b, dims=NN):
    return lax.dot_general(a, b, dims, preferred_element_type=jnp.float32)


def unit(size):
    return (iota((size, size), 0) == iota((size, size), 1)).astype(jnp.bfloat16)


def clip_bounds(lengths_ref):
    bounds = []
    end = jnp.int32(0)
    for c in range(lengths_ref.shape[0]):
        start = end
        end = end + lengths_ref[c]
        bounds.append((start, end))
    return bounds


def split_kernel(devices, me_ref, key_ref, value_ref, kept_ref, given_ref):
    half = key_ref.shape[1] // 2
    low, high = slice(0, half), slice(half, 2 * half)
    side = place_of(me_ref[0], devices)[0]

    @pl.when(side == 0)
    def _():
        kept_ref[:, low] = key_ref[:, low]
        kept_ref[:, high] = value_ref[:, low]
        given_ref[:, low] = key_ref[:, high]
        given_ref[:, high] = value_ref[:, high]

    @pl.when(side != 0)
    def _():
        kept_ref[:, low] = key_ref[:, high]
        kept_ref[:, high] = value_ref[:, high]
        given_ref[:, low] = key_ref[:, low]
        given_ref[:, high] = value_ref[:, low]


def pack_kernel(plane, lengths_ref, owner_ref, slot_ref, query_ref, out_ref):
    rows, width = query_ref.shape
    half = width // 2
    ring = plane // 2
    owner = owner_ref[...]
    slot = slot_ref[...]
    place = owner * rows + slot
    clip = jnp.zeros_like(place)
    for _, end in clip_bounds(lengths_ref):
        clip = clip + (place >= end).astype(jnp.int32)
    clip = jnp.broadcast_to(clip.astype(jnp.float32), (8, rows))
    square = (rows, rows)
    along = jnp.broadcast_to(owner.astype(jnp.float32), square)
    earlier = (along == along.T) & (iota(square, 0) < iota(square, 1))
    rank = jnp.sum(earlier.astype(jnp.float32), axis=0, keepdims=True).astype(jnp.int32)
    there = lax.div(lax.rem(owner, plane), 2)
    which = lax.div(owner, plane) * 2 + lax.rem(owner, 2)
    target = there * MSG + which * BOUND + rank
    spread = (ring * MSG, rows)
    line = iota(spread, 0)
    lane = iota(spread, 1)
    kind = lax.rem(line, MSG)
    pick = (line == target).astype(jnp.bfloat16)
    main = dot(pick, query_ref[...])
    slot_down = jnp.broadcast_to((slot + 1).astype(jnp.float32), square).T
    slots = jnp.where(iota(square, 1) == rows - 1, slot_down, 0.0).astype(jnp.bfloat16)
    meta = dot(pick, slots)
    meta = jnp.where((kind == 0) & (lane < rows // 2), clip[:1], meta)
    turned = pltpu.roll(clip, rows // 2, 1)[:1]
    meta = jnp.where((kind == 1) & (lane < rows // 2), turned, meta).astype(jnp.bfloat16)
    for s in range(2):
        at = slice(s * ring * MSG, (s + 1) * ring * MSG)
        out_ref[at, :half] = main[:, s * half : (s + 1) * half].astype(jnp.bfloat16)
        out_ref[at, half:] = meta


def place_of(me, devices):
    plane = devices // 2
    half = lax.div(me, plane)
    return half, lax.div(lax.rem(me, plane), 2), lax.rem(me, 2)


def key_sources(me, devices):
    plane = devices // 2
    ring = plane // 2
    half, y, core = place_of(me, devices)

    def pair(h, distance):
        there = lax.rem(y + (2 * core - 1) * distance + ring, ring)
        at = h * plane + there * 2
        return [at, at + 1]

    near, far = half, 1 - half
    order = [me, lax.rem(me + plane, devices)]
    for h, distance in ((near, 1), (far, 1), (near, 2), (far, 2), (near, 3), (far, 3)):
        order += pair(h, distance)
    return order + [pair(near, 4)[0] + core, pair(far, 4)[0] + core]


def unpack_kernel(
    devices,
    counts,
    me_ref,
    lengths_ref,
    got_ref,
    other_ref,
    far_query_ref,
    near_query_ref,
    *refs,
):
    *clip_refs, dead_ref = refs
    each = got_ref.shape[0]
    lines = 2 * each
    rows = HEAD_DIM
    plane = devices // 2
    me = me_ref[0]
    half, _, core = place_of(me, devices)
    got = jnp.concatenate([got_ref[...], other_ref[...]], axis=0)
    data, meta = got[:, :-rows], got[:, -rows:]
    kind = lax.rem(iota((lines, 1), 0), MSG)
    from_half = lax.div(kind, 2 * BOUND)
    from_core = lax.rem(lax.div(kind, BOUND), 2)
    quarter = (from_half == half).astype(jnp.int32) * 2 + (from_core != core).astype(jnp.int32)
    slot = meta[:, rows - 1 :].astype(jnp.float32)
    target = jnp.where(slot > 0, slot - 1.0 + (quarter * rows).astype(jnp.float32), -1.0)
    target = jnp.broadcast_to(target, (lines, rows))
    target = jnp.concatenate(
        [target[i : i + rows, :].T[:1, :] for i in range(0, lines, rows)], axis=1
    )
    put = (iota((4 * rows, lines), 0).astype(jnp.float32) == target).astype(jnp.bfloat16)
    queries = dot(put, data).astype(jnp.bfloat16)
    far_query_ref[...] = queries[: 2 * rows]
    near_query_ref[...] = queries[2 * rows :]

    order = key_sources(me, devices)
    slots = len(order)
    block = (slots, lines)
    line = iota(block, 0)
    source = jnp.zeros(block, jnp.int32)
    for j, at in enumerate(order):
        at = lax.div(at, 2) * MSG + (lax.rem(at, 2) != core).astype(jnp.int32) * each
        source = jnp.where(line == j, at, source)
    first = dot((source == iota(block, 1)).astype(jnp.bfloat16), meta)
    second = dot((source + 1 == iota(block, 1)).astype(jnp.bfloat16), meta)
    ids = jnp.where(iota((slots, rows), 1) < rows // 2, first, pltpu.roll(second, rows // 2, 1))
    down = iota((rows, rows), 0).astype(jnp.float32)
    for j in range(slots):
        member = (ids[j : j + 1, :] == down).astype(jnp.bfloat16)
        clips = dot(unit(rows), member, NT).astype(jnp.bfloat16)
        call = 0
        while j >= sum(counts[: call + 1]):
            call += 1
        at = (j - sum(counts[:call])) * rows
        clip_refs[call][at : at + rows, :] = clips

    bounds = clip_bounds(lengths_ref)
    other = lax.rem(me + plane, devices)
    away = 1 - 2 * core
    lane = iota((rows, HEAD_DIM), 1)
    for q, owner in enumerate((other, other + away, me, me + away)):
        position = iota((rows, HEAD_DIM), 0) + owner * rows
        dead = jnp.zeros((rows, HEAD_DIM), jnp.float32)
        for c, (start, end) in enumerate(bounds):
            outside = (position < start) | (position >= end)
            dead = jnp.where((lane == c) & outside, MASKED, dead)
        dead_ref[q * rows : (q + 1) * rows, :] = dead.astype(jnp.bfloat16)


def split3(value):
    high = value.astype(jnp.bfloat16)
    rest = value - high.astype(jnp.float32)
    mid = rest.astype(jnp.bfloat16)
    low = (rest - mid.astype(jnp.float32)).astype(jnp.bfloat16)
    return high, mid, low


def pair_up(sizes):
    chunks = []
    at = 0
    parts = []
    for i, size in enumerate(sizes):
        if size >= CHUNK:
            for start in range(0, size, CHUNK):
                chunks.append((at, [(i, start, CHUNK)]))
                at += CHUNK
            continue
        parts.append((i, 0, size))
        if sum(p[2] for p in parts) == CHUNK:
            chunks.append((at, parts))
            at += CHUNK
            parts = []
    assert not parts
    return chunks


def attend_kernel(tiles, sizes, first, last, *refs):
    refs = list(refs)
    dead_ref = refs.pop(0)
    query_refs = [refs.pop(0) for _ in range(tiles)]
    block_refs = [refs.pop(0) for _ in sizes]
    clip_ref = refs.pop(0)
    if not first:
        sum_ref, stat_ref = refs.pop(0), refs.pop(0)
    if last:
        out_ref, level_ref, sent_ref = refs.pop(0), refs.pop(0), refs.pop(0)
    else:
        new_sum_ref, new_stat_ref = refs.pop(0), refs.pop(0)
    scores = refs.pop(0)
    tile, width = query_refs[0].shape
    heads = width // HEAD_DIM
    lane = iota((tile, HEAD_DIM), 1)
    chunks = pair_up(sizes)
    ones = jnp.ones((CHUNK, HEAD_DIM), jnp.bfloat16)
    stats = [jnp.zeros((tile, HEAD_DIM), jnp.float32) for _ in range(tiles)]

    def columns(h):
        return slice(h * HEAD_DIM, (h + 1) * HEAD_DIM)

    def score(t, h):
        rows = slice(t * tile, (t + 1) * tile)
        query = jnp.concatenate([query_refs[t][:, columns(h)], dead_ref[rows, :]], axis=1)
        top = jnp.full((tile, HEAD_DIM), -3e38, jnp.float32)
        for at, members in chunks:
            key = jnp.concatenate([block_refs[i][o : o + n, columns(h)] for i, o, n in members])
            key = jnp.concatenate([key, clip_ref[at : at + CHUNK, :]], axis=1)
            s = dot(query, key, NT)
            scores[t * heads + h, :, at : at + CHUNK] = s
            for j in range(0, CHUNK, HEAD_DIM):
                top = jnp.maximum(top, s[:, j : j + HEAD_DIM])
        return top

    def finish(t, h, top):
        rows = slice(t * tile, (t + 1) * tile)
        top = jnp.max(top, axis=1, keepdims=True) * SCALE2
        if first:
            total = jnp.zeros((tile, 2 * HEAD_DIM), jnp.float32)
        else:
            old_top = stat_ref[rows, h : h + 1]
            top = jnp.maximum(top, old_top)
            fade = jnp.exp2(old_top - top)
            weight = stat_ref[rows, h + 8 : h + 9] * fade
            weight = jnp.broadcast_to(weight, (tile, HEAD_DIM))
            total = jnp.concatenate([sum_ref[rows, columns(h)] * fade, weight], axis=1)
        for at, members in chunks:
            w = scores[t * heads + h, :, at : at + CHUNK] * SCALE2 - top
            w = jnp.exp2(w).astype(jnp.bfloat16)
            value = jnp.concatenate(
                [block_refs[i][o : o + n, columns(heads + h)] for i, o, n in members]
            )
            total = total + dot(w, jnp.concatenate([value, ones], axis=1))
        weight = total[:, HEAD_DIM:]
        if not last:
            new_sum_ref[rows, columns(h)] = total[:, :HEAD_DIM]
            stats[t] = jnp.where(lane == h, top, stats[t])
            stats[t] = jnp.where(lane == h + 8, weight, stats[t])
            return
        out = total[:, :HEAD_DIM] / weight
        stats[t] = jnp.where(lane == h, top + jnp.log2(weight), stats[t])
        out_ref[:, columns(h)] = out[: tile // 2]
        sent_ref[:, columns(h)] = out[tile // 2 :].astype(jnp.bfloat16)

    jobs = [(t, h) for t in range(tiles) for h in range(heads)]
    ahead = score(*jobs[0])
    for n, job in enumerate(jobs):
        top = ahead
        if n + 1 < len(jobs):
            ahead = score(*jobs[n + 1])
        finish(*job, top)
    if not last:
        for t in range(tiles):
            new_stat_ref[t * tile : (t + 1) * tile, :] = stats[t]
        return
    level_ref[...] = stats[0][: tile // 2]
    lane = lane[tile // 2 :]
    high, mid, low = split3(stats[0][tile // 2 :])
    mid = pltpu.roll(mid.astype(jnp.float32), 8, 1)
    low = pltpu.roll(low.astype(jnp.float32), 16, 1)
    packed = jnp.where(lane < 8, high.astype(jnp.float32), jnp.where(lane < 16, mid, low))
    sent_ref[:, width:] = packed.astype(jnp.bfloat16)


def combine_kernel(
    devices, which, me_ref, lengths_ref, own_ref, level_ref, got_ref, gates_ref, out_ref
):
    rows, width = own_ref.shape
    me = me_ref[0]
    half, _, core = place_of(me, devices)
    owner = lax.rem(me + (1 - which) * (devices // 2), devices)
    other = pl.multiple_of((1 - core) * rows, rows)
    got = got_ref[pl.ds(other, rows), :]
    lane = iota((rows, HEAD_DIM), 1)
    position = iota((rows, HEAD_DIM), 0) + owner * rows
    member = jnp.zeros((rows, HEAD_DIM), jnp.float32)
    for c, (start, end) in enumerate(clip_bounds(lengths_ref)):
        inside = (position >= start) & (position < end)
        member = jnp.where((lane == c) & inside, 1.0, member)
    gates = jnp.where(half == 0, gates_ref[:, :width], gates_ref[:, width:])
    gate = dot(member[:, : gates.shape[0]].astype(jnp.bfloat16), gates)
    stat = got[:, width:].astype(jnp.float32)
    for h in range(width // HEAD_DIM):
        got_level = (stat[:, h : h + 1] + stat[:, h + 8 : h + 9]) + stat[:, h + 16 : h + 17]
        gap = level_ref[:, h : h + 1] - got_level
        own_share = 1.0 / (1.0 + jnp.exp2(-gap))
        got_share = 1.0 / (1.0 + jnp.exp2(gap))
        at = slice(h * HEAD_DIM, (h + 1) * HEAD_DIM)
        mixed = own_ref[:, at] * own_share + got[:, at].astype(jnp.float32) * got_share
        out_ref[:, at] = (mixed * gate[:, at]).astype(jnp.bfloat16)


def join_kernel(devices, me_ref, mine_ref, back_ref, out_ref):
    half = mine_ref.shape[1]
    low, high = slice(0, half), slice(half, 2 * half)
    side = place_of(me_ref[0], devices)[0]

    @pl.when(side == 0)
    def _():
        out_ref[:, low] = mine_ref[...]
        out_ref[:, high] = back_ref[...]

    @pl.when(side != 0)
    def _():
        out_ref[:, low] = back_ref[...]
        out_ref[:, high] = mine_ref[...]


SMEM = pl.BlockSpec(memory_space=pltpu.SMEM)


def whole(shape):
    return pl.BlockSpec(shape, lambda i: (0,) * len(shape))


def call(kernel, operands, in_specs, outs, behind=(), scratch=(), vmem=None, token=False, cost=0):
    taken, extra = len(operands), len(behind)

    def body(*refs):
        ins, rest = refs[:taken], list(refs[taken + extra :])
        if token:
            done = rest.pop(len(outs))
            done[...] = jnp.zeros(done.shape, done.dtype)
        kernel(*ins, *rest)

    results = list(outs) + ([jax.ShapeDtypeStruct((8, HEAD_DIM), jnp.float32)] if token else [])
    return pl.pallas_call(
        body,
        grid=(1,),
        in_specs=list(in_specs) + [pl.BlockSpec(memory_space=pl.ANY)] * extra,
        out_specs=[whole(o.shape) for o in results],
        out_shape=results,
        scratch_shapes=scratch,
        compiler_params=pltpu.CompilerParams(vmem_limit_bytes=vmem),
        cost_estimate=pl.CostEstimate(flops=0, bytes_accessed=cost, transcendentals=0),
    )(*operands, *behind)


def unpack_attend_kernel(devices, counts, sizes, *refs):
    refs = list(refs)
    head, blocks = [refs.pop(0) for _ in range(4)], [refs.pop(0) for _ in sizes]
    far_query, near_query, later_clips, dead, sums, stats, clips, scores = refs
    unpack_kernel(devices, counts, *head, far_query, near_query, clips, later_clips, dead)
    attend_kernel(
        2, sizes, True, False, dead, far_query, near_query, *blocks, clips, sums, stats, scores
    )


def unpack_attend(devices, counts, me, lengths, got, other, blocks, behind=()):
    sent_rows, sent_width = got.shape
    width = sent_width - HEAD_DIM
    sizes = [b.shape[0] for b in blocks]
    tile, rows = 2 * HEAD_DIM, 4 * HEAD_DIM
    operands = [me, lengths, got, other, *blocks]
    first, second = (c * HEAD_DIM for c in counts)
    return call(
        functools.partial(unpack_attend_kernel, devices, counts, sizes),
        operands,
        [SMEM, SMEM] + [whole(o.shape) for o in operands[2:]],
        [jax.ShapeDtypeStruct((tile, width), jnp.bfloat16)] * 2
        + [
            jax.ShapeDtypeStruct((second, HEAD_DIM), jnp.bfloat16),
            jax.ShapeDtypeStruct((rows, HEAD_DIM), jnp.bfloat16),
            jax.ShapeDtypeStruct((rows, width), jnp.float32),
            jax.ShapeDtypeStruct((rows, HEAD_DIM), jnp.float32),
        ],
        behind,
        [
            pltpu.VMEM((first, HEAD_DIM), jnp.bfloat16),
            pltpu.VMEM((2 * width // HEAD_DIM, tile, sum(sizes)), jnp.float32),
        ],
        ATTEND_VMEM,
    )


def attend_last(which, dead, queries, blocks, clips, state, behind=()):
    query = queries[which]
    tile, width = query.shape
    sizes = [b.shape[0] for b in blocks]

    def part(array):
        return pl.BlockSpec((tile, array.shape[1]), lambda i: (which, 0))

    return call(
        functools.partial(attend_kernel, 1, sizes, False, True),
        [dead, query, *blocks, clips, *state],
        [part(dead), whole(query.shape)]
        + [whole(b.shape) for b in blocks]
        + [whole(clips.shape)]
        + [part(s) for s in state],
        [
            jax.ShapeDtypeStruct((tile // 2, width), jnp.float32),
            jax.ShapeDtypeStruct((tile // 2, HEAD_DIM), jnp.float32),
            jax.ShapeDtypeStruct((tile // 2, width + HEAD_DIM), jnp.bfloat16),
        ],
        behind,
        [pltpu.VMEM((width // HEAD_DIM, tile, sum(sizes)), jnp.float32)],
        ATTEND_VMEM,
    )


def shards(
    query_rows, key_rows, value_rows, deal_owner, deal_slot, clip_lengths, clip_steps, gate_table
):
    devices = lax.axis_size("seq")
    plane = devices // 2
    ring = plane // 2
    rows, width = query_rows.shape
    half_width = width // 2
    me = lax.axis_index("seq")
    core = me % 2

    def index(h, y, c):
        return h * plane + (y % ring) * 2 + c

    everyone = [(h, y, c) for h in range(2) for y in range(ring) for c in range(2)]
    to_half = [(index(h, y, c), index(1 - h, y, c)) for h, y, c in everyone]
    to_core = [(index(h, y, c), index(h, y, 1 - c)) for h, y, c in everyone]
    to_next = [(index(h, y, c), index(h, y + 1 - 2 * c, c)) for h, y, c in everyone]
    to_second = [(index(h, y, c), index(h, y + 2 - 4 * c, c)) for h, y, c in everyone]
    chips = [[2 * i, 2 * i + 1] for i in range(plane)]

    def step(block):
        return lax.ppermute(block, "seq", to_next)

    def chip_gather(block):
        return lax.all_gather(block, "seq", axis_index_groups=chips, tiled=True)

    def core_half(block):
        return lax.dynamic_slice_in_dim(block, core * rows, rows, axis=0)

    def bf16(*shape):
        return jax.ShapeDtypeStruct(shape, jnp.bfloat16)

    mine = me[None]
    sent_rows = plane * MSG
    sent_width = half_width + HEAD_DIM
    kept, given = call(
        functools.partial(split_kernel, devices),
        [mine, key_rows, value_rows],
        [SMEM, whole((rows, width)), whole((rows, width))],
        [bf16(rows, width)] * 2,
    )
    taken = lax.ppermute(given, "seq", to_half)
    (message,) = call(
        functools.partial(pack_kernel, plane),
        [clip_lengths, deal_owner[None, :], deal_slot[None, :], query_rows],
        [SMEM, whole((1, rows)), whole((1, rows)), whole((rows, width))],
        [bf16(sent_rows, sent_width)],
        [given],
        cost=8 * 1024 * 1024,
    )
    kept, message = lax.optimization_barrier((kept, message))
    near0 = chip_gather(kept)
    got = lax.all_to_all(
        message.reshape(plane, MSG, sent_width),
        "seq",
        split_axis=0,
        concat_axis=0,
        axis_index_groups=[list(range(c, devices, 2)) for c in range(2)],
        tiled=True,
    ).reshape(sent_rows, sent_width)

    near1 = step(near0)
    far1 = step(chip_gather(taken))
    near2 = step(near1)
    far2 = step(far1)
    near2, got = lax.optimization_barrier((near2, got))
    near3 = step(near2)
    far3 = step(far2)
    near4 = step(core_half(near3))
    gates = jnp.take(gate_table, clip_steps, axis=0)
    counts = (12, 4)
    far4 = lax.ppermute(core_half(far2), "seq", to_second)
    *queries, clips1, dead, sums, stats = unpack_attend(
        devices,
        counts,
        mine,
        clip_lengths,
        got,
        lax.ppermute(got, "seq", to_core),
        [kept, taken, near1, far1, near2, far2, near3],
        [gates],
    )
    state = (sums, stats)

    def finish(which, behind):
        own, level, sent = attend_last(
            which, dead, queries, [far3, near4, far4], clips1, state, behind
        )
        operands = [mine, clip_lengths, own, level, chip_gather(sent), gates]
        return call(
            functools.partial(combine_kernel, devices, which),
            operands,
            [SMEM, SMEM] + [whole(o.shape) for o in operands[2:]],
            [bf16(rows, half_width)],
            vmem=SMALL_VMEM,
        )[0]

    theirs = finish(0, [])
    back = lax.ppermute(theirs, "seq", to_half)
    ours = finish(1, [theirs])
    return call(
        functools.partial(join_kernel, devices),
        [mine, ours, back],
        [SMEM, whole((rows, half_width)), whole((rows, half_width))],
        [bf16(rows, width)],
        vmem=SMALL_VMEM,
    )[0]


def solution(mesh):
    placed = (
        P(("dp", "seq"), "tensor"),
        P(("dp", "seq"), "tensor"),
        P(("dp", "seq"), "tensor"),
        P(("dp", "seq")),
        P(("dp", "seq")),
        P("dp"),
        P("dp"),
        P(None, "tensor"),
    )
    return jax.shard_map(
        shards, mesh=mesh, in_specs=placed, out_specs=P(("dp", "seq"), "tensor"), check_vma=False
    )
```

```python
import functools
import math

import jax
import jax.numpy as jnp
from jax import lax
from jax.experimental import pallas as pl
from jax.experimental.pallas import tpu as pltpu
from jax.sharding import PartitionSpec as P

HEAD_DIM = 128
MASKED = -1e30
SCALE2 = math.log2(math.e) / math.sqrt(HEAD_DIM)
BOUND = 6
MSG = 24
CHUNK = 256
ATTEND_VMEM = 30 * 1024 * 1024
SMALL_VMEM = 10 * 1024 * 1024

NN = (((1,), (0,)), ((), ()))
NT = (((1,), (1,)), ((), ()))
TN = (((0,), (0,)), ((), ()))


def iota(shape, axis):
    return lax.broadcasted_iota(jnp.int32, shape, axis)


def dot(a, b, dims=NN):
    return lax.dot_general(a, b, dims, preferred_element_type=jnp.float32)


def unit(size):
    return (iota((size, size), 0) == iota((size, size), 1)).astype(jnp.bfloat16)


def clip_bounds(lengths_ref):
    bounds = []
    end = jnp.int32(0)
    for c in range(lengths_ref.shape[0]):
        start = end
        end = end + lengths_ref[c]
        bounds.append((start, end))
    return bounds


def split_kernel(devices, me_ref, key_ref, value_ref, kept_ref, given_ref):
    half = key_ref.shape[1] // 2
    low, high = slice(0, half), slice(half, 2 * half)
    side = place_of(me_ref[0], devices)[0]

    @pl.when(side == 0)
    def _():
        kept_ref[:, low] = key_ref[:, low]
        kept_ref[:, high] = value_ref[:, low]
        given_ref[:, low] = key_ref[:, high]
        given_ref[:, high] = value_ref[:, high]

    @pl.when(side != 0)
    def _():
        kept_ref[:, low] = key_ref[:, high]
        kept_ref[:, high] = value_ref[:, high]
        given_ref[:, low] = key_ref[:, low]
        given_ref[:, high] = value_ref[:, low]


def pack_kernel(plane, lengths_ref, owner_ref, slot_ref, query_ref, out_ref):
    rows, width = query_ref.shape
    half = width // 2
    ring = plane // 2
    owner = owner_ref[...]
    slot = slot_ref[...]
    place = owner * rows + slot
    clip = jnp.zeros_like(place)
    for _, end in clip_bounds(lengths_ref):
        clip = clip + (place >= end).astype(jnp.int32)
    clip = jnp.broadcast_to(clip.astype(jnp.float32), (8, rows))
    square = (rows, rows)
    along = jnp.broadcast_to(owner.astype(jnp.float32), square)
    earlier = (along == along.T) & (iota(square, 0) < iota(square, 1))
    rank = jnp.sum(earlier.astype(jnp.float32), axis=0, keepdims=True).astype(jnp.int32)
    there = lax.div(lax.rem(owner, plane), 2)
    which = lax.div(owner, plane) * 2 + lax.rem(owner, 2)
    target = there * MSG + which * BOUND + rank
    spread = (ring * MSG, rows)
    line = iota(spread, 0)
    lane = iota(spread, 1)
    kind = lax.rem(line, MSG)
    pick = (line == target).astype(jnp.bfloat16)
    main = dot(pick, query_ref[...])
    slot_down = jnp.broadcast_to((slot + 1).astype(jnp.float32), square).T
    slots = jnp.where(iota(square, 1) == rows - 1, slot_down, 0.0).astype(jnp.bfloat16)
    meta = dot(pick, slots)
    meta = jnp.where((kind == 0) & (lane < rows // 2), clip[:1], meta)
    turned = pltpu.roll(clip, rows // 2, 1)[:1]
    meta = jnp.where((kind == 1) & (lane < rows // 2), turned, meta).astype(jnp.bfloat16)
    for s in range(2):
        at = slice(s * ring * MSG, (s + 1) * ring * MSG)
        out_ref[at, :half] = main[:, s * half : (s + 1) * half].astype(jnp.bfloat16)
        out_ref[at, half:] = meta


def place_of(me, devices):
    plane = devices // 2
    half = lax.div(me, plane)
    return half, lax.div(lax.rem(me, plane), 2), lax.rem(me, 2)


def key_sources(me, devices):
    plane = devices // 2
    ring = plane // 2
    half, y, core = place_of(me, devices)

    def pair(h, distance):
        there = lax.rem(y + (2 * core - 1) * distance + ring, ring)
        at = h * plane + there * 2
        return [at, at + 1]

    near, far = half, 1 - half
    order = [me, lax.rem(me + plane, devices)]
    for h, distance in ((near, 1), (far, 1), (near, 2), (far, 2), (near, 3), (far, 3)):
        order += pair(h, distance)
    return order + [pair(near, 4)[0] + core, pair(far, 4)[0] + core]


def unpack_kernel(
    devices,
    counts,
    me_ref,
    lengths_ref,
    got_ref,
    other_ref,
    far_query_ref,
    near_query_ref,
    *refs,
):
    *clip_refs, dead_ref = refs
    each = got_ref.shape[0]
    lines = 2 * each
    rows = HEAD_DIM
    plane = devices // 2
    me = me_ref[0]
    half, _, core = place_of(me, devices)
    got = jnp.concatenate([got_ref[...], other_ref[...]], axis=0)
    data, meta = got[:, :-rows], got[:, -rows:]
    kind = lax.rem(iota((lines, 1), 0), MSG)
    from_half = lax.div(kind, 2 * BOUND)
    from_core = lax.rem(lax.div(kind, BOUND), 2)
    quarter = (from_half == half).astype(jnp.int32) * 2 + (from_core != core).astype(jnp.int32)
    slot = meta[:, rows - 1 :].astype(jnp.float32)
    target = jnp.where(slot > 0, slot - 1.0 + (quarter * rows).astype(jnp.float32), -1.0)
    target = jnp.broadcast_to(target, (lines, rows))
    target = jnp.concatenate(
        [target[i : i + rows, :].T[:1, :] for i in range(0, lines, rows)], axis=1
    )
    put = (iota((4 * rows, lines), 0).astype(jnp.float32) == target).astype(jnp.bfloat16)
    queries = dot(put, data).astype(jnp.bfloat16)
    far_query_ref[...] = queries[: 2 * rows]
    near_query_ref[...] = queries[2 * rows :]

    order = key_sources(me, devices)
    slots = len(order)
    block = (slots, lines)
    line = iota(block, 0)
    source = jnp.zeros(block, jnp.int32)
    for j, at in enumerate(order):
        at = lax.div(at, 2) * MSG + (lax.rem(at, 2) != core).astype(jnp.int32) * each
        source = jnp.where(line == j, at, source)
    first = dot((source == iota(block, 1)).astype(jnp.bfloat16), meta)
    second = dot((source + 1 == iota(block, 1)).astype(jnp.bfloat16), meta)
    ids = jnp.where(iota((slots, rows), 1) < rows // 2, first, pltpu.roll(second, rows // 2, 1))
    down = iota((rows, rows), 0).astype(jnp.float32)
    for j in range(slots):
        member = (ids[j : j + 1, :] == down).astype(jnp.bfloat16)
        clips = dot(unit(rows), member, NT).astype(jnp.bfloat16)
        call = 0
        while j >= sum(counts[: call + 1]):
            call += 1
        at = (j - sum(counts[:call])) * rows
        clip_refs[call][at : at + rows, :] = clips

    bounds = clip_bounds(lengths_ref)
    other = lax.rem(me + plane, devices)
    away = 1 - 2 * core
    lane = iota((rows, HEAD_DIM), 1)
    for q, owner in enumerate((other, other + away, me, me + away)):
        position = iota((rows, HEAD_DIM), 0) + owner * rows
        dead = jnp.zeros((rows, HEAD_DIM), jnp.float32)
        for c, (start, end) in enumerate(bounds):
            outside = (position < start) | (position >= end)
            dead = jnp.where((lane == c) & outside, MASKED, dead)
        dead_ref[q * rows : (q + 1) * rows, :] = dead.astype(jnp.bfloat16)


def split3(value):
    high = value.astype(jnp.bfloat16)
    rest = value - high.astype(jnp.float32)
    mid = rest.astype(jnp.bfloat16)
    low = (rest - mid.astype(jnp.float32)).astype(jnp.bfloat16)
    return high, mid, low


def pair_up(sizes):
    chunks = []
    at = 0
    parts = []
    for i, size in enumerate(sizes):
        if size >= CHUNK:
            for start in range(0, size, CHUNK):
                chunks.append((at, [(i, start, CHUNK)]))
                at += CHUNK
            continue
        parts.append((i, 0, size))
        if sum(p[2] for p in parts) == CHUNK:
            chunks.append((at, parts))
            at += CHUNK
            parts = []
    assert not parts
    return chunks


def attend_kernel(tiles, sizes, first, last, *refs):
    refs = list(refs)
    dead_ref = refs.pop(0)
    query_refs = [refs.pop(0) for _ in range(tiles)]
    block_refs = [refs.pop(0) for _ in sizes]
    clip_ref = refs.pop(0)
    if not first:
        sum_ref, stat_ref = refs.pop(0), refs.pop(0)
    if last:
        out_ref, level_ref, sent_ref = refs.pop(0), refs.pop(0), refs.pop(0)
    else:
        new_sum_ref, new_stat_ref = refs.pop(0), refs.pop(0)
    scores = refs.pop(0)
    tile, width = query_refs[0].shape
    heads = width // HEAD_DIM
    lane = iota((tile, HEAD_DIM), 1)
    chunks = pair_up(sizes)
    ones = jnp.ones((CHUNK, HEAD_DIM), jnp.bfloat16)
    stats = [jnp.zeros((tile, HEAD_DIM), jnp.float32) for _ in range(tiles)]

    def columns(h):
        return slice(h * HEAD_DIM, (h + 1) * HEAD_DIM)

    def score(t, h):
        rows = slice(t * tile, (t + 1) * tile)
        query = jnp.concatenate([query_refs[t][:, columns(h)], dead_ref[rows, :]], axis=1)
        top = jnp.full((tile, HEAD_DIM), -3e38, jnp.float32)
        for at, members in chunks:
            key = jnp.concatenate([block_refs[i][o : o + n, columns(h)] for i, o, n in members])
            key = jnp.concatenate([key, clip_ref[at : at + CHUNK, :]], axis=1)
            s = dot(query, key, NT)
            scores[t * heads + h, :, at : at + CHUNK] = s
            for j in range(0, CHUNK, HEAD_DIM):
                top = jnp.maximum(top, s[:, j : j + HEAD_DIM])
        return top

    def finish(t, h, top):
        rows = slice(t * tile, (t + 1) * tile)
        top = jnp.max(top, axis=1, keepdims=True) * SCALE2
        if first:
            total = jnp.zeros((tile, 2 * HEAD_DIM), jnp.float32)
        else:
            old_top = stat_ref[rows, h : h + 1]
            top = jnp.maximum(top, old_top)
            fade = jnp.exp2(old_top - top)
            weight = stat_ref[rows, h + 8 : h + 9] * fade
            weight = jnp.broadcast_to(weight, (tile, HEAD_DIM))
            total = jnp.concatenate([sum_ref[rows, columns(h)] * fade, weight], axis=1)
        for at, members in chunks:
            w = scores[t * heads + h, :, at : at + CHUNK] * SCALE2 - top
            w = jnp.exp2(w).astype(jnp.bfloat16)
            value = jnp.concatenate(
                [block_refs[i][o : o + n, columns(heads + h)] for i, o, n in members]
            )
            total = total + dot(w, jnp.concatenate([value, ones], axis=1))
        weight = total[:, HEAD_DIM:]
        if not last:
            new_sum_ref[rows, columns(h)] = total[:, :HEAD_DIM]
            stats[t] = jnp.where(lane == h, top, stats[t])
            stats[t] = jnp.where(lane == h + 8, weight, stats[t])
            return
        out = total[:, :HEAD_DIM] / weight
        stats[t] = jnp.where(lane == h, top + jnp.log2(weight), stats[t])
        out_ref[:, columns(h)] = out[: tile // 2]
        sent_ref[:, columns(h)] = out[tile // 2 :].astype(jnp.bfloat16)

    jobs = [(t, h) for t in range(tiles) for h in range(heads)]
    ahead = score(*jobs[0])
    for n, job in enumerate(jobs):
        top = ahead
        if n + 1 < len(jobs):
            ahead = score(*jobs[n + 1])
        finish(*job, top)
    if not last:
        for t in range(tiles):
            new_stat_ref[t * tile : (t + 1) * tile, :] = stats[t]
        return
    level_ref[...] = stats[0][: tile // 2]
    lane = lane[tile // 2 :]
    high, mid, low = split3(stats[0][tile // 2 :])
    mid = pltpu.roll(mid.astype(jnp.float32), 8, 1)
    low = pltpu.roll(low.astype(jnp.float32), 16, 1)
    packed = jnp.where(lane < 8, high.astype(jnp.float32), jnp.where(lane < 16, mid, low))
    sent_ref[:, width:] = packed.astype(jnp.bfloat16)


def combine_kernel(
    devices, which, me_ref, lengths_ref, own_ref, level_ref, got_ref, gates_ref, out_ref
):
    rows, width = own_ref.shape
    me = me_ref[0]
    half, _, core = place_of(me, devices)
    owner = lax.rem(me + (1 - which) * (devices // 2), devices)
    other = pl.multiple_of((1 - core) * rows, rows)
    got = got_ref[pl.ds(other, rows), :]
    lane = iota((rows, HEAD_DIM), 1)
    position = iota((rows, HEAD_DIM), 0) + owner * rows
    member = jnp.zeros((rows, HEAD_DIM), jnp.float32)
    for c, (start, end) in enumerate(clip_bounds(lengths_ref)):
        inside = (position >= start) & (position < end)
        member = jnp.where((lane == c) & inside, 1.0, member)
    gates = jnp.where(half == 0, gates_ref[:, :width], gates_ref[:, width:])
    gate = dot(member[:, : gates.shape[0]].astype(jnp.bfloat16), gates)
    stat = got[:, width:].astype(jnp.float32)
    for h in range(width // HEAD_DIM):
        got_level = (stat[:, h : h + 1] + stat[:, h + 8 : h + 9]) + stat[:, h + 16 : h + 17]
        gap = level_ref[:, h : h + 1] - got_level
        own_share = 1.0 / (1.0 + jnp.exp2(-gap))
        got_share = 1.0 / (1.0 + jnp.exp2(gap))
        at = slice(h * HEAD_DIM, (h + 1) * HEAD_DIM)
        mixed = own_ref[:, at] * own_share + got[:, at].astype(jnp.float32) * got_share
        out_ref[:, at] = (mixed * gate[:, at]).astype(jnp.bfloat16)


def join_kernel(devices, me_ref, mine_ref, back_ref, out_ref):
    half = mine_ref.shape[1]
    low, high = slice(0, half), slice(half, 2 * half)
    side = place_of(me_ref[0], devices)[0]

    @pl.when(side == 0)
    def _():
        out_ref[:, low] = mine_ref[...]
        out_ref[:, high] = back_ref[...]

    @pl.when(side != 0)
    def _():
        out_ref[:, low] = back_ref[...]
        out_ref[:, high] = mine_ref[...]


SMEM = pl.BlockSpec(memory_space=pltpu.SMEM)


def whole(shape):
    return pl.BlockSpec(shape, lambda i: (0,) * len(shape))


def call(kernel, operands, in_specs, outs, behind=(), scratch=(), vmem=None, token=False, cost=0):
    taken, extra = len(operands), len(behind)

    def body(*refs):
        ins, rest = refs[:taken], list(refs[taken + extra :])
        if token:
            done = rest.pop(len(outs))
            done[...] = jnp.zeros(done.shape, done.dtype)
        kernel(*ins, *rest)

    results = list(outs) + ([jax.ShapeDtypeStruct((8, HEAD_DIM), jnp.float32)] if token else [])
    return pl.pallas_call(
        body,
        grid=(1,),
        in_specs=list(in_specs) + [pl.BlockSpec(memory_space=pl.ANY)] * extra,
        out_specs=[whole(o.shape) for o in results],
        out_shape=results,
        scratch_shapes=scratch,
        compiler_params=pltpu.CompilerParams(vmem_limit_bytes=vmem),
        cost_estimate=pl.CostEstimate(flops=0, bytes_accessed=cost, transcendentals=0),
    )(*operands, *behind)


def unpack_attend_kernel(devices, counts, sizes, *refs):
    refs = list(refs)
    head, blocks = [refs.pop(0) for _ in range(4)], [refs.pop(0) for _ in sizes]
    far_query, near_query, later_clips, dead, sums, stats, clips, scores = refs
    unpack_kernel(devices, counts, *head, far_query, near_query, clips, later_clips, dead)
    attend_kernel(
        2, sizes, True, False, dead, far_query, near_query, *blocks, clips, sums, stats, scores
    )


def unpack_attend(devices, counts, me, lengths, got, other, blocks, behind=()):
    sent_rows, sent_width = got.shape
    width = sent_width - HEAD_DIM
    sizes = [b.shape[0] for b in blocks]
    tile, rows = 2 * HEAD_DIM, 4 * HEAD_DIM
    operands = [me, lengths, got, other, *blocks]
    first, second = (c * HEAD_DIM for c in counts)
    return call(
        functools.partial(unpack_attend_kernel, devices, counts, sizes),
        operands,
        [SMEM, SMEM] + [whole(o.shape) for o in operands[2:]],
        [jax.ShapeDtypeStruct((tile, width), jnp.bfloat16)] * 2
        + [
            jax.ShapeDtypeStruct((second, HEAD_DIM), jnp.bfloat16),
            jax.ShapeDtypeStruct((rows, HEAD_DIM), jnp.bfloat16),
            jax.ShapeDtypeStruct((rows, width), jnp.float32),
            jax.ShapeDtypeStruct((rows, HEAD_DIM), jnp.float32),
        ],
        behind,
        [
            pltpu.VMEM((first, HEAD_DIM), jnp.bfloat16),
            pltpu.VMEM((2 * width // HEAD_DIM, tile, sum(sizes)), jnp.float32),
        ],
        ATTEND_VMEM,
    )


def attend_last(which, dead, queries, blocks, clips, state, behind=()):
    query = queries[which]
    tile, width = query.shape
    sizes = [b.shape[0] for b in blocks]

    def part(array):
        return pl.BlockSpec((tile, array.shape[1]), lambda i: (which, 0))

    return call(
        functools.partial(attend_kernel, 1, sizes, False, True),
        [dead, query, *blocks, clips, *state],
        [part(dead), whole(query.shape)]
        + [whole(b.shape) for b in blocks]
        + [whole(clips.shape)]
        + [part(s) for s in state],
        [
            jax.ShapeDtypeStruct((tile // 2, width), jnp.float32),
            jax.ShapeDtypeStruct((tile // 2, HEAD_DIM), jnp.float32),
            jax.ShapeDtypeStruct((tile // 2, width + HEAD_DIM), jnp.bfloat16),
        ],
        behind,
        [pltpu.VMEM((width // HEAD_DIM, tile, sum(sizes)), jnp.float32)],
        ATTEND_VMEM,
    )


def shards(
    query_rows, key_rows, value_rows, deal_owner, deal_slot, clip_lengths, clip_steps, gate_table
):
    devices = lax.axis_size("seq")
    plane = devices // 2
    ring = plane // 2
    rows, width = query_rows.shape
    half_width = width // 2
    me = lax.axis_index("seq")
    core = me % 2

    def index(h, y, c):
        return h * plane + (y % ring) * 2 + c

    everyone = [(h, y, c) for h in range(2) for y in range(ring) for c in range(2)]
    to_half = [(index(h, y, c), index(1 - h, y, c)) for h, y, c in everyone]
    to_core = [(index(h, y, c), index(h, y, 1 - c)) for h, y, c in everyone]
    to_next = [(index(h, y, c), index(h, y + 1 - 2 * c, c)) for h, y, c in everyone]
    to_second = [(index(h, y, c), index(h, y + 2 - 4 * c, c)) for h, y, c in everyone]
    chips = [[2 * i, 2 * i + 1] for i in range(plane)]

    def step(block):
        return lax.ppermute(block, "seq", to_next)

    def chip_gather(block):
        return lax.all_gather(block, "seq", axis_index_groups=chips, tiled=True)

    def core_half(block):
        return lax.dynamic_slice_in_dim(block, core * rows, rows, axis=0)

    def bf16(*shape):
        return jax.ShapeDtypeStruct(shape, jnp.bfloat16)

    mine = me[None]
    sent_rows = plane * MSG
    sent_width = half_width + HEAD_DIM
    kept, given = call(
        functools.partial(split_kernel, devices),
        [mine, key_rows, value_rows],
        [SMEM, whole((rows, width)), whole((rows, width))],
        [bf16(rows, width)] * 2,
    )
    taken = lax.ppermute(given, "seq", to_half)
    (message,) = call(
        functools.partial(pack_kernel, plane),
        [clip_lengths, deal_owner[None, :], deal_slot[None, :], query_rows],
        [SMEM, whole((1, rows)), whole((1, rows)), whole((rows, width))],
        [bf16(sent_rows, sent_width)],
        [given],
        cost=8 * 1024 * 1024,
    )
    kept, message = lax.optimization_barrier((kept, message))
    near0 = chip_gather(kept)
    got = lax.all_to_all(
        message.reshape(plane, MSG, sent_width),
        "seq",
        split_axis=0,
        concat_axis=0,
        axis_index_groups=[list(range(c, devices, 2)) for c in range(2)],
        tiled=True,
    ).reshape(sent_rows, sent_width)

    near1 = step(near0)
    far1 = step(chip_gather(taken))
    near2 = step(near1)
    far2 = step(far1)
    gates = jnp.take(gate_table, clip_steps, axis=0)
    near2, got, gates = lax.optimization_barrier((near2, got, gates))
    near3 = step(near2)
    far3 = step(far2)
    near4 = step(core_half(near3))
    counts = (12, 4)
    far4 = lax.ppermute(core_half(far2), "seq", to_second)
    *queries, clips1, dead, sums, stats = unpack_attend(
        devices,
        counts,
        mine,
        clip_lengths,
        got,
        lax.ppermute(got, "seq", to_core),
        [kept, taken, near1, far1, near2, far2, near3],
        [gates],
    )
    state = (sums, stats)

    def finish(which, behind):
        own, level, sent = attend_last(
            which, dead, queries, [far3, near4, far4], clips1, state, behind
        )
        operands = [mine, clip_lengths, own, level, chip_gather(sent), gates]
        return call(
            functools.partial(combine_kernel, devices, which),
            operands,
            [SMEM, SMEM] + [whole(o.shape) for o in operands[2:]],
            [bf16(rows, half_width)],
            vmem=SMALL_VMEM,
        )[0]

    theirs = finish(0, [])
    back = lax.ppermute(theirs, "seq", to_half)
    ours = finish(1, [theirs])
    return call(
        functools.partial(join_kernel, devices),
        [mine, ours, back],
        [SMEM, whole((rows, half_width)), whole((rows, half_width))],
        [bf16(rows, width)],
        vmem=SMALL_VMEM,
    )[0]


def solution(mesh):
    placed = (
        P(("dp", "seq"), "tensor"),
        P(("dp", "seq"), "tensor"),
        P(("dp", "seq"), "tensor"),
        P(("dp", "seq")),
        P(("dp", "seq")),
        P("dp"),
        P("dp"),
        P(None, "tensor"),
    )
    return jax.shard_map(
        shards, mesh=mesh, in_specs=placed, out_specs=P(("dp", "seq"), "tensor"), check_vma=False
    )
```
